512 devices in a mesh: atoms: 32 (over x_hi, z, core), kvec: 16 (over x_lo, y).
Axes of the slice: x: 4 (x_hi: 2, x_lo: 2; x = x_hi * 2 + x_lo), y: 8, z: 8, core: 2. Of those that a mesh axis runs over, the one named last changes fastest.
Arguments:
- positions: float32 [3, 65536], P(None, 'atoms'), may hold values from 0 to 1
- feats: float32 [64, 65536], P(None, 'atoms'), may hold values from -6 to 6
- species: int32 [65536], P('atoms'), may hold values from 0 to 15
- pad_count: int32 [256], P('atoms'), may hold values from 128 to 256
- k_lattice: int32 [3, 4096], P(None, 'kvec'), may hold values from -12 to 13, as said below
- filter_width: float32 [64], replicated, may hold values from 2e-05 to 0.002
- w_charge: float32 [64, 64], replicated, may hold values from -0.75 to 0.75
- species_embed: float32 [64, 16], replicated, may hold values from -3 to 3
- w_out: float32 [64, 64], replicated, may hold values from -0.75 to 0.75
- grad_out: float32 [64, 65536], P(None, ('atoms', 'kvec')), may hold values from -6 to 6
Outputs:
- message: float32 [64, 65536], P(None, ('atoms', 'kvec'))
- grad_positions: float32 [3, 65536], P(None, ('atoms', 'kvec'))
- grad_feats: float32 [64, 65536], P(None, ('atoms', 'kvec'))
The draws below stay inside these ranges and needn't reach their ends.
Inputs may be any that keep to these rules, and one draw needn't show every extreme that they name: `k_lattice`: the 4096 columns are distinct nonzero integer vectors k with k[0] > 0, or k[0] = 0 and k[1] > 0, or k[0] = k[1] = 0 and k[2] > 0, and with squared length at most 169.
All inputs are finite; a program needn't handle non-finite values.
Results may differ from the reference program's by a relative error of at most 0.0003.
Values sent between devices are 32-bit elements; how exact they have to be, the bound alone decides.
A program may use at most 64 MiB of HBM per device.

```python
import math
import jax
import jax.numpy as jnp
from jax import lax

C = 64
NSPEC = 16
NATOM = 65536
NBLK = 256
KVEC = 4096


def draw_k_lattice(key, part):
    key = jax.random.fold_in(key, 7)
    extremes = [[13, 0, 0], [0, 1, -12]]
    others = []
    for comp_one in range(-13, 14):
        for comp_two in range(-13, 14):
            for comp_three in range(-13, 14):
                upper = comp_one > 0 or (comp_one == 0 and comp_two > 0) or (comp_one == 0 and comp_two == 0 and (comp_three > 0))
                inside = comp_one * comp_one + comp_two * comp_two + comp_three * comp_three <= 169
                point = [comp_one, comp_two, comp_three]
                if upper and inside and (point not in extremes):
                    others.append(point)
    lattice_table = jnp.asarray(extremes + others, jnp.int32).T
    other_count = len(others)
    key_one, key_two = jax.random.split(key)
    shuffled = jax.random.permutation(key_one, other_count)[:KVEC - 2] + 2
    chosen = jnp.concatenate([jnp.arange(2, dtype=jnp.int32), shuffled.astype(jnp.int32)])
    chosen = jax.random.permutation(key_two, chosen)
    return jnp.take(lattice_table, chosen, axis=1)


def plant(entries, stream_key, smallest, top_value):
    extent = entries.shape
    place = [jax.random.randint(jax.random.fold_in(stream_key, axis), (), 0, extent[axis]) for axis in range(len(extent))]
    entries = entries.at[tuple(place)].set(smallest)
    longest = extent.index(max(extent))
    place[longest] = (place[longest] + 1) % extent[longest]
    return entries.at[tuple(place)].set(top_value)


def block_scale(rng, dims, cuts, least, top_value):
    def one(dim, parts):
        steps = jax.random.uniform(jax.random.fold_in(jax.random.fold_in(rng, 6), dim), (parts,), jnp.float32, least / len(cuts), top_value / len(cuts))
        return jnp.repeat(jnp.exp(steps), dims[dim] // parts).reshape((-1,) + (1,) * (len(dims) - dim - 1))

    loudness = one(*cuts[0])
    for cut in cuts[1:]:
        loudness = loudness * one(*cut)
    return loudness


def noise(stream_key, dims, spread, limit, cuts=(), held_as=jnp.bfloat16):
    loudness = block_scale(stream_key, dims, cuts, -0.22, 0.18) if cuts else 1.0
    entries = jax.random.normal(stream_key, dims, jnp.float32) * spread * loudness
    return jnp.minimum(jnp.maximum(entries, -limit), limit).astype(held_as)


def setup_inputs(seed: int = 0) -> dict:
    arg_keys = jax.random.split(jax.random.key(seed), 11)
    positions = jnp.clip(1.0 * jax.random.uniform(arg_keys[0], (3, NATOM), jnp.float32) ** block_scale(arg_keys[0], (3, NATOM), ((1, 32),), -0.2, 0.2), 0.0, 1.0)
    feats = noise(arg_keys[1], (C, NATOM), 1.0, 6.0, ((1, 32),), jnp.float32)
    species = plant(jax.random.randint(arg_keys[2], (NATOM,), 0, NSPEC), jax.random.fold_in(arg_keys[2], 1), 0, NSPEC - 1).astype(jnp.int32)
    pad_count = plant(jax.random.randint(arg_keys[3], (NBLK,), 128, 257), jax.random.fold_in(arg_keys[3], 1), 128, 256).astype(jnp.int32)
    k_lattice = draw_k_lattice(jax.random.fold_in(arg_keys[10], 71), 0)
    filter_width = jnp.clip(jnp.exp(jax.random.uniform(arg_keys[5], (C,), jnp.float32, math.log(1.9999999494757503e-05), math.log(0.002))), 1.9999999494757503e-05, 0.002)
    w_charge = noise(arg_keys[6], (C, C), C ** -0.5, 0.75, (), jnp.float32)
    species_embed = noise(arg_keys[7], (C, NSPEC), 0.5, 3.0, (), jnp.float32)
    w_out = noise(arg_keys[8], (C, C), C ** -0.5, 0.75, (), jnp.float32)
    grad_out = noise(arg_keys[9], (C, NATOM), 1.0, 6.0, ((1, 512),), jnp.float32)
    return {"positions": positions, "feats": feats, "species": species, "pad_count": pad_count, "k_lattice": k_lattice, "filter_width": filter_width, "w_charge": w_charge, "species_embed": species_embed, "w_out": w_out, "grad_out": grad_out}


exact = lax.Precision.HIGHEST
two_pi = 2.0 * math.pi

def reference(positions, feats, species, pad_count, k_lattice, filter_width, w_charge, species_embed, w_out, grad_out):
    block = 2048
    block_count = NATOM // block
    valid_mask = (jnp.arange(NATOM) % 256 < jnp.repeat(pad_count, 256)).astype(jnp.float32)
    charges = valid_mask[None, :] * (jnp.dot(w_charge.T, feats, precision=exact) + species_embed[:, species])
    wave_vec = two_pi * k_lattice.astype(jnp.float32)
    k_square = lax.optimization_barrier(jnp.sum(wave_vec * wave_vec, axis=0))
    filter_gain = jnp.exp(-k_square[:, None] * filter_width[None, :]) * 40.0 / (k_square[:, None] + 40.0) / math.sqrt(NATOM)

    def blocks(array):
        return array.reshape(array.shape[0], block_count, block).transpose(1, 0, 2)

    def unblock(array):
        return array.transpose(1, 0, 2).reshape(array.shape[1], NATOM)
    pos_blocks = blocks(positions)
    charge_blocks = blocks(charges)
    mask_blocks = valid_mask.reshape(block_count, block)
    cot_blocks = blocks(grad_out)

    def trig(pos_block):
        phase = jnp.dot(pos_block.T, wave_vec, precision=exact)
        return (jnp.cos(phase), jnp.sin(phase))

    def pass_one(carry, items):
        pos_block, charge_block = items
        cos_tile, sine_tile = trig(pos_block)
        part_cos = jnp.einsum('aj,ca->jc', cos_tile, charge_block, precision=exact)
        part_sin = jnp.einsum('aj,ca->jc', sine_tile, charge_block, precision=exact)
        return ((carry[0] + part_cos, carry[1] + part_sin), jnp.float32(0.0))
    zero_kc = jnp.zeros((KVEC, C), jnp.float32)
    (sf_cos, sf_sin), _ = lax.scan(pass_one, (zero_kc, zero_kc), (pos_blocks, charge_blocks))
    h_cos = filter_gain * sf_cos
    h_sin = filter_gain * sf_sin

    def pass_two(carry, items):
        pos_block, mask_block, cot_block = items
        cos_tile, sine_tile = trig(pos_block)
        field_out = mask_block[None, :] * (jnp.einsum('aj,jc->ca', cos_tile, h_cos, precision=exact) + jnp.einsum('aj,jc->ca', sine_tile, h_sin, precision=exact))
        message = jnp.dot(w_out.T, field_out, precision=exact)
        adjoint = mask_block[None, :] * jnp.dot(w_out, cot_block, precision=exact)
        part_cos = jnp.einsum('aj,ca->jc', cos_tile, adjoint, precision=exact)
        part_sin = jnp.einsum('aj,ca->jc', sine_tile, adjoint, precision=exact)
        return ((carry[0] + part_cos, carry[1] + part_sin), (message, adjoint))
    (e_cos, e_sin), (message_blocks, adjoint_blocks) = lax.scan(pass_two, (zero_kc, zero_kc), (pos_blocks, mask_blocks, cot_blocks))
    b_cos = filter_gain * e_cos
    b_sin = filter_gain * e_sin

    def pass_three(carry, items):
        pos_block, charge_block, mask_block, adjoint = items
        cos_tile, sine_tile = trig(pos_block)
        charge_grad = jnp.einsum('aj,jc->ca', cos_tile, b_cos, precision=exact) + jnp.einsum('aj,jc->ca', sine_tile, b_sin, precision=exact)
        feat_grad = jnp.dot(w_charge, mask_block[None, :] * charge_grad, precision=exact)
        along_sin = jnp.einsum('ca,jc->aj', adjoint, h_sin, precision=exact) + jnp.einsum('ca,jc->aj', charge_block, b_sin, precision=exact)
        along_cos = jnp.einsum('ca,jc->aj', adjoint, h_cos, precision=exact) + jnp.einsum('ca,jc->aj', charge_block, b_cos, precision=exact)
        dphase = cos_tile * along_sin - sine_tile * along_cos
        force_part = jnp.einsum('xj,aj->xa', wave_vec, dphase, precision=exact)
        return (carry, (force_part, feat_grad))
    _, (force_blocks, feat_blocks) = lax.scan(pass_three, jnp.float32(0.0), (pos_blocks, charge_blocks, mask_blocks, adjoint_blocks))
    return (unblock(message_blocks), unblock(force_blocks), unblock(feat_blocks))
```

```python
import functools
import math

import jax
import jax.numpy as jnp
import numpy as np
from jax import lax
from jax.experimental import pallas as pl
from jax.experimental.pallas import tpu as pltpu
from jax.sharding import PartitionSpec as P

MESH = pl.DeviceIdType.MESH
exact = lax.Precision.HIGHEST
two_pi = 2.0 * math.pi
f32 = jnp.float32
bf16 = jnp.bfloat16

A = 1024
K = 512
H = 256
CH = 64
S = 128


def fit_poly(fn, count, points=2000):
    nodes = 0.25 * (np.cos(np.pi * (np.arange(points) + 0.5) / points) + 1.0) * 0.5
    table = np.vander(nodes / 0.25, count, increasing=True)
    coef = np.linalg.lstsq(table, fn(np.sqrt(nodes)), rcond=None)[0]
    return [float(c) / 0.25**n for n, c in enumerate(coef)]


sin_coef = fit_poly(lambda u: 2.0 * np.sin(np.pi * u) / u, 5)
cos_coef = fit_poly(lambda u: np.cos(np.pi * u), 5)


def horner(coef, sq):
    total = coef[-1]
    for c in coef[-2::-1]:
        total = total * sq + c
    return total


def sin_cos_turns(t):
    u = t - jnp.round(t)
    sq = u * u
    twice_sin = u * horner(sin_coef, sq)
    cos_half = horner(cos_coef, sq)
    return 1.0 - 0.5 * (twice_sin * twice_sin), twice_sin * cos_half


def split(value):
    high = value.astype(bf16)
    return high, (value - high.astype(f32)).astype(bf16)


def dot(a, b, dims=((1,), (0,)), precision=None):
    return lax.dot_general(a, b, (dims, ((), ())), precision=precision, preferred_element_type=f32)


def middle_out(i, n):
    return n // 2 + ((i + 1) // 2) * (1 - 2 * (i % 2))


def kernel(
    pos_ref, feats_ref, species_ref, pad_ref, k_ref, width_ref, wq_ref, embed_ref, wo_ref, grad_ref,
    message_ref, force_ref, gfeat_ref,
    feats, kall, kcol, kmat, xmat, mask, t_hi, t_lo, cos_f, sin_f, charge, cots, adjoint,
    part, core_in, core_sum, ring_in, owned, table, out_y, in_y, out_f, in_f,
    feats_sem, k_sem, cot_send, cot_recv, core_sem, plane_send, plane_recv, table_send, table_recv,
    y_send, y_recv, f_send, f_recv,
):
    atoms_at = lax.axis_index("atoms")
    kvec_at = lax.axis_index("kvec")
    core, z, x_hi = atoms_at % 2, (atoms_at // 2) % 8, atoms_at // 16
    x_lo, y = kvec_at // 8, kvec_at % 8
    x = x_hi * 2 + x_lo
    me = x * 8 + z

    def on_y(other):
        return (atoms_at, x_lo * 8 + other)

    def on_plane(px, pz):
        return ((px // 2) * 16 + pz * 2 + core, (px % 2) * 8 + y)

    sibling = (atoms_at + 1 - 2 * core, kvec_at)
    partner = (atoms_at, (1 - x_lo) * 8 + y)

    def plane_loop(body):
        def step(i, _):
            px = (x + middle_out(i // 8, 4)) % 4
            pz = (z + middle_out(i % 8, 8)) % 8
            body(px, pz, px * 8 + pz)
            return 0

        lax.fori_loop(0, 31, step, 0)

    def y_loop(body):
        def step(i, _):
            body((y + middle_out(i, 8)) % 8)
            return 0

        lax.fori_loop(0, 7, step, 0)

    def remote(src, dst, send, recv, device):
        return pltpu.make_async_remote_copy(
            src_ref=src, dst_ref=dst, send_sem=send, recv_sem=recv, device_id=device, device_id_type=MESH
        )

    barrier = pltpu.get_barrier_semaphore()

    def greet(device):
        pl.semaphore_signal(barrier, inc=1, device_id=device, device_id_type=MESH)

    plane_loop(lambda px, pz, p: greet(on_plane(px, pz)))
    y_loop(lambda other: greet(on_y(other)))
    greet(sibling)

    feats_copy = pltpu.make_async_copy(
        feats_ref.at[:, pl.ds(pl.multiple_of(x_lo * A, A), A)], feats, feats_sem
    )
    feats_copy.start()

    kall[x_lo] = jnp.concatenate([k_ref[...].astype(f32), jnp.zeros((5, H), f32)], axis=0)
    pos = pos_ref[:, pl.ds(pl.multiple_of(x_lo * A, A), A)]
    pos = jnp.concatenate([pos, jnp.zeros((5, A), f32)], axis=0)
    pos_hi = pos.astype(bf16).astype(f32)
    pos_mid = (pos - pos_hi).astype(bf16).astype(f32)
    pos_low = (pos - pos_hi) - pos_mid
    xmat[...] = jnp.concatenate([pos_hi, pos_mid, pos_low, jnp.zeros((8, A), f32)], axis=0).astype(bf16)
    lanes = lax.broadcasted_iota(jnp.int32, (1, 256), 1)
    for block in range(4):
        mask[:, block * 256 : (block + 1) * 256] = (lanes < pad_ref[x_lo * 4 + block]).astype(f32)

    def trig_half(q):
        kt = kall[q].T
        kcol[pl.ds(pl.multiple_of(q * H, H), H), :] = kt
        kmat[pl.ds(pl.multiple_of(q * H, H), H), :] = jnp.concatenate([kt] * 4, axis=1).astype(bf16)

        def step(i, _):
            rows = pl.ds(pl.multiple_of(q * H + i * 32, 32), 32)
            rows_sin = pl.ds(pl.multiple_of(K + q * H + i * 32, 32), 32)
            left = kmat[rows, :]
            for part_at in range(4):
                cols = slice(part_at * 256, (part_at + 1) * 256)
                cos, sin = sin_cos_turns(dot(left, xmat[:, cols]))
                cos_f[rows, cols] = cos
                sin_f[rows, cols] = sin
                high, low = split(cos)
                t_hi[rows, cols] = high
                t_lo[rows, cols] = low
                high, low = split(sin)
                t_hi[rows_sin, cols] = high
                t_lo[rows_sin, cols] = low
            return 0

        lax.fori_loop(0, H // 32, step, 0)

    low_lanes = lax.broadcasted_iota(jnp.int32, (1, 128), 1) < CH

    def factors(which, q, quant):
        both = quant[...]
        for i in range(2):
            base = q * H + i * 128
            found = []
            for offset in (0, K):
                rows = pl.ds(pl.multiple_of(offset + base, 128), 128)
                one = dot(t_hi[rows, :], both, ((1,), (1,))) + dot(t_lo[rows, :], both, ((1,), (1,)))
                found.append(one + pltpu.roll(one, CH, 1))
            part[which, pl.ds(pl.multiple_of(base, 128), 128), :] = jnp.where(low_lanes, found[0], found[1])

    trig_half(x_lo)

    feats_copy.wait()
    one_hot = (
        lax.broadcasted_iota(jnp.int32, (16, A), 0) == species_ref[:, pl.ds(pl.multiple_of(x_lo * A, A), A)]
    ).astype(f32)
    q_high, q_low = split(
        mask[...]
        * (
            dot(wq_ref[...], feats[...], ((0,), (0,)), exact)
            + dot(embed_ref[...], one_hot, precision=exact)
        )
    )
    charge[0:CH, :] = q_high
    charge[CH:128, :] = q_low
    factors(0, x_lo, charge)

    pl.semaphore_wait(barrier, 39)

    k_copy = remote(kall.at[x_lo], kall.at[x_lo], k_sem.at[0], k_sem.at[1], partner)
    k_copy.start()

    def cot_copy(other, slot):
        return remote(grad_ref, cots.at[slot], cot_send.at[other], cot_recv.at[slot], on_y(other))

    y_loop(lambda other: cot_copy(other, y).start())
    cots[y] = grad_ref[...]

    remote(kall.at[1 - x_lo], kall.at[1 - x_lo], k_sem.at[0], k_sem.at[1], partner).wait_recv()
    trig_half(1 - x_lo)
    factors(0, 1 - x_lo, charge)

    def core_copy(which, stage, src, dst):
        return remote(src, dst, core_sem.at[0, which, stage], core_sem.at[1, which, stage], sibling)

    own_rows = pl.ds(pl.multiple_of(core * H, H), H)
    other_rows = pl.ds(pl.multiple_of((1 - core) * H, H), H)

    def pair_sum_copy(which):
        return core_copy(which, 0, part.at[which, other_rows, :], core_in.at[which])

    def share_rows(p):
        return pl.ds(pl.multiple_of(p * 8, 8), 8)

    def plane_copy(which, px, pz, p, slot):
        return remote(
            core_sum.at[which, share_rows(p), :], ring_in.at[which, slot],
            plane_send.at[which, p], plane_recv.at[which, slot], on_plane(px, pz),
        )

    def scatter_start(which):
        pair_sum_copy(which).wait_recv()
        core_sum[which] = part[which, own_rows, :] + core_in[which]
        plane_loop(lambda px, pz, p: plane_copy(which, px, pz, p, me).start())
        ring_in[which, me] = core_sum[which, share_rows(me), :]

    def table_rows(p):
        return pl.ds(pl.multiple_of(core * H + p * 8, 8), 8)

    def table_copy(which, px, pz, p, slot):
        return remote(
            owned.at[which], table.at[which, table_rows(slot), :],
            table_send.at[which, p], table_recv.at[which, slot], on_plane(px, pz),
        )

    def gather_start(which):
        plane_loop(lambda px, pz, p: plane_copy(which, px, pz, p, p).wait_recv())
        total = ring_in[which, 0]
        for p in range(1, 32):
            total = total + ring_in[which, p]
        wave = two_pi * kcol[table_rows(me), :]
        square = jnp.sum(wave * wave, axis=1, keepdims=True)
        width = width_ref[...]
        width = jnp.concatenate([width, width], axis=1)
        gain = jnp.exp(-square * width) * 40.0 / (square + 40.0) / 256.0
        owned[which] = gain * total
        plane_loop(lambda px, pz, p: table_copy(which, px, pz, p, me).start())
        table[which, table_rows(me), :] = owned[which]

    def pair_share_copy(which, rows):
        return core_copy(which, 1, table.at[which, rows, :], table.at[which, rows, :])

    def gather_end(which):
        plane_loop(lambda px, pz, p: table_copy(which, px, pz, p, p).wait_recv())
        pair_share_copy(which, own_rows).start()
        pair_share_copy(which, other_rows).wait_recv()

    pair_sum_copy(0).start()
    scatter_start(0)

    y_loop(lambda other: cot_copy(other, other).wait_recv())
    for s in range(8):
        cols = slice(s * S, (s + 1) * S)
        high, low = split(mask[:, cols] * dot(wo_ref[...], cots[s], precision=exact))
        adjoint[0:CH, cols] = high
        adjoint[CH:128, cols] = low
    factors(1, 0, adjoint)
    factors(1, 1, adjoint)
    pair_sum_copy(1).start()
    scatter_start(1)

    gather_start(0)
    gather_start(1)

    def y_copy(which, other, slot):
        return remote(
            out_y.at[which, other], in_y.at[which, slot], y_send.at[which, other], y_recv.at[which, slot], on_y(other)
        )

    def fields(which):
        high, low = split(table[which].T)
        left = jnp.concatenate(
            [
                jnp.concatenate([high[0:CH], high[CH:128]], axis=1),
                jnp.concatenate([low[0:CH], low[CH:128]], axis=1),
            ],
            axis=0,
        )
        for at in range(4):
            cols = slice(at * 256, (at + 1) * 256)
            both = dot(left, t_hi[:, cols]) + dot(left, t_lo[:, cols])
            field = both[0:CH] + both[CH:128]
            out_y[which, 2 * at] = field[:, 0:S]
            out_y[which, 2 * at + 1] = field[:, S:256]
        y_loop(lambda other: y_copy(which, other, y).start())
        in_y[which, y] = out_y[which, y]

    def forces(which, quant, add):
        high, low = split(table[which])
        high, low = high.astype(f32), low.astype(f32)
        sin_side = jnp.where(low_lanes, pltpu.roll(high, CH, 1), low).astype(bf16)
        cos_side = jnp.where(low_lanes, high, pltpu.roll(low, CH, 1)).astype(bf16)
        sin_side = jnp.concatenate([sin_side, sin_side], axis=1)
        cos_side = jnp.concatenate([cos_side, cos_side], axis=1)
        columns = [kcol[:, n : n + 1] for n in range(3)]
        for at in range(4):
            cols = slice(at * 256, (at + 1) * 256)
            high_q, low_q = quant[0:CH, cols], quant[CH:128, cols]
            right = jnp.concatenate([high_q, high_q, low_q, low_q], axis=0)
            turn = cos_f[:, cols] * dot(sin_side, right) - sin_f[:, cols] * dot(cos_side, right)
            rows = [jnp.sum(column * turn, axis=0, keepdims=True) for column in columns]
            rows = jnp.concatenate(rows + [jnp.zeros((5, 256), f32)], axis=0)
            for half in range(2):
                slot = 2 * at + half
                here = rows[:, half * S : (half + 1) * S]
                out_f[slot] = out_f[slot] + here if add else here

    def f_copy(other, slot):
        return remote(out_f.at[other], in_f.at[slot], f_send.at[other], f_recv.at[slot], on_y(other))

    gather_end(0)
    fields(0)
    forces(0, adjoint, False)
    gather_end(1)
    fields(1)
    forces(1, charge, True)
    y_loop(lambda other: f_copy(other, y).start())
    in_f[y] = out_f[y]

    share = mask[:, pl.ds(pl.multiple_of(y * S, S), S)]

    def collect(which):
        y_loop(lambda other: y_copy(which, other, other).wait_recv())
        total = in_y[which, 0]
        for s in range(1, 8):
            total = total + in_y[which, s]
        return share * total

    message_ref[...] = dot(wo_ref[...], collect(0), ((0,), (0,)), exact)
    gfeat_ref[...] = dot(wq_ref[...], collect(1), precision=exact)
    y_loop(lambda other: f_copy(other, other).wait_recv())
    total = in_f[0]
    for s in range(1, 8):
        total = total + in_f[s]
    force_ref[...] = (two_pi * total)[0:3, :]

    k_copy.wait_send()
    y_loop(lambda other: cot_copy(other, y).wait_send())
    for which in range(2):
        pair_sum_copy(which).wait_send()
        pair_share_copy(which, own_rows).wait_send()
        plane_loop(lambda px, pz, p: plane_copy(which, px, pz, p, me).wait_send())
        plane_loop(lambda px, pz, p: table_copy(which, px, pz, p, me).wait_send())
        y_loop(lambda other: y_copy(which, other, y).wait_send())
    y_loop(lambda other: f_copy(other, y).wait_send())


def on_device(
    positions, feats, species, pad_count, k_lattice, filter_width, w_charge, species_embed, w_out, grad_out
):
    vmem = pl.BlockSpec(memory_space=pltpu.VMEM)
    dma = pltpu.SemaphoreType.DMA
    return pl.pallas_call(
        kernel,
        out_shape=(
            jax.ShapeDtypeStruct((CH, S), f32),
            jax.ShapeDtypeStruct((3, S), f32),
            jax.ShapeDtypeStruct((CH, S), f32),
        ),
        in_specs=[
            vmem,
            pl.BlockSpec(memory_space=pl.ANY),
            vmem,
            pl.BlockSpec(memory_space=pltpu.SMEM),
            vmem, vmem, vmem, vmem, vmem, vmem,
        ],
        out_specs=(vmem, vmem, vmem),
        scratch_shapes=[
            pltpu.VMEM((CH, A), f32),
            pltpu.VMEM((2, 8, H), f32),
            pltpu.VMEM((K, 8), f32),
            pltpu.VMEM((K, 32), bf16),
            pltpu.VMEM((32, A), bf16),
            pltpu.VMEM((1, A), f32),
            pltpu.VMEM((2 * K, A), bf16),
            pltpu.VMEM((2 * K, A), bf16),
            pltpu.VMEM((K, A), f32),
            pltpu.VMEM((K, A), f32),
            pltpu.VMEM((128, A), bf16),
            pltpu.VMEM((8, CH, S), f32),
            pltpu.VMEM((128, A), bf16),
            pltpu.VMEM((2, K, 128), f32),
            pltpu.VMEM((2, H, 128), f32),
            pltpu.VMEM((2, H, 128), f32),
            pltpu.VMEM((2, 32, 8, 128), f32),
            pltpu.VMEM((2, 8, 128), f32),
            pltpu.VMEM((2, K, 128), f32),
            pltpu.VMEM((2, 8, CH, S), f32),
            pltpu.VMEM((2, 8, CH, S), f32),
            pltpu.VMEM((8, 8, S), f32),
            pltpu.VMEM((8, 8, S), f32),
            dma, dma((2,)), dma((8,)), dma((8,)), dma((2, 2, 2)),
            dma((2, 32)), dma((2, 32)), dma((2, 32)), dma((2, 32)),
            dma((2, 8)), dma((2, 8)), dma((8,)), dma((8,)),
        ],
        name="ewald",
        compiler_params=pltpu.CompilerParams(
            collective_id=0, has_side_effects=True, vmem_limit_bytes=40 * 1024 * 1024
        ),
    )(
        positions, feats, species.reshape(1, -1), pad_count, k_lattice, filter_width.reshape(1, -1),
        w_charge, species_embed, w_out, grad_out,
    )


def solution(mesh):
    placed = (
        P(None, "atoms"),
        P(None, "atoms"),
        P("atoms"),
        P("atoms"),
        P(None, "kvec"),
        P(),
        P(),
        P(),
        P(),
        P(None, ("atoms", "kvec")),
    )
    return jax.shard_map(
        on_device,
        mesh=mesh,
        in_specs=placed,
        out_specs=(P(None, ("atoms", "kvec")),) * 3,
        check_vma=False,
    )
```

```python
import functools
import math

import jax
import jax.numpy as jnp
import numpy as np
from jax import lax
from jax.experimental import pallas as pl
from jax.experimental.pallas import tpu as pltpu
from jax.sharding import PartitionSpec as P

MESH = pl.DeviceIdType.MESH
exact = lax.Precision.HIGHEST
two_pi = 2.0 * math.pi
f32 = jnp.float32
bf16 = jnp.bfloat16

A = 1024
K = 512
H = 256
CH = 64
S = 128


def fit_poly(fn, count, points=2000):
    nodes = 0.25 * (np.cos(np.pi * (np.arange(points) + 0.5) / points) + 1.0) * 0.5
    table = np.vander(nodes / 0.25, count, increasing=True)
    coef = np.linalg.lstsq(table, fn(np.sqrt(nodes)), rcond=None)[0]
    return [float(c) / 0.25**n for n, c in enumerate(coef)]


sin_coef = fit_poly(lambda u: 2.0 * np.sin(np.pi * u) / u, 5)
cos_coef = fit_poly(lambda u: np.cos(np.pi * u), 5)


def horner(coef, sq):
    total = coef[-1]
    for c in coef[-2::-1]:
        total = total * sq + c
    return total


def sin_cos_turns(t):
    u = t - jnp.round(t)
    sq = u * u
    twice_sin = u * horner(sin_coef, sq)
    cos_half = horner(cos_coef, sq)
    return 1.0 - 0.5 * (twice_sin * twice_sin), twice_sin * cos_half


def split(value):
    high = value.astype(bf16)
    return high, (value - high.astype(f32)).astype(bf16)


def dot(a, b, dims=((1,), (0,)), precision=None):
    return lax.dot_general(a, b, (dims, ((), ())), precision=precision, preferred_element_type=f32)


def far_first(n):
    return sorted(range(1, n), key=lambda d: -min(d, n - d))


plane_steps = sorted(
    [(dx, dz) for dx in range(4) for dz in range(8) if dx or dz],
    key=lambda d: -(min(d[0], 4 - d[0]) + min(d[1], 8 - d[1])),
)


def kernel(
    pos_hbm, feats_hbm, species_hbm, pad_hbm, k_hbm, width_hbm, wq_hbm, embed_hbm, wo_hbm, grad_hbm,
    message_ref, force_ref, gfeat_ref,
    pos_ref, feats, species_ref, pad_ref, k_ref, width_ref, wq_ref, embed_ref, wo_ref, grad_ref,
    kall, kcol, kmat, xmat, mask, t_hi, t_lo, cos_f, sin_f, charge, cots, adjoint,
    part, core_in, core_sum, ring_in, owned, table, out_y, in_y, out_f, in_f,
    load_sem, k_sem, cot_sem, core_sem, plane_sem, table_sem, y_sem, f_sem,
):
    atoms_at = lax.axis_index("atoms")
    kvec_at = lax.axis_index("kvec")
    core, z, x_hi = atoms_at % 2, (atoms_at // 2) % 8, atoms_at // 16
    x_lo, y = kvec_at // 8, kvec_at % 8
    x = x_hi * 2 + x_lo
    me = x * 8 + z

    ys = [(y + d) % 8 for d in far_first(8)]
    y_peers = [(other, (atoms_at, x_lo * 8 + other)) for other in ys]
    plane_peers = []
    for dx, dz in plane_steps:
        px, pz = (x + dx) % 4, (z + dz) % 8
        plane_peers.append((px * 8 + pz, ((px // 2) * 16 + pz * 2 + core, (px % 2) * 8 + y)))
    sibling = (atoms_at + 1 - 2 * core, kvec_at)
    partner = (atoms_at, (1 - x_lo) * 8 + y)

    barrier = pltpu.get_barrier_semaphore()
    for device in [d for _, d in y_peers] + [d for _, d in plane_peers] + [sibling]:
        pl.semaphore_signal(barrier, inc=1, device_id=device, device_id_type=MESH)

    half_atoms = pl.ds(pl.multiple_of(x_lo * A, A), A)
    loads = {}
    for n, (name, src, dst) in enumerate([
        ("k", k_hbm, k_ref),
        ("pos", pos_hbm, pos_ref),
        ("pad", pad_hbm, pad_ref),
        ("feats", feats_hbm.at[:, half_atoms], feats),
        ("species", species_hbm, species_ref),
        ("wq", wq_hbm, wq_ref),
        ("embed", embed_hbm, embed_ref),
        ("grad", grad_hbm, grad_ref),
        ("wo", wo_hbm, wo_ref),
        ("width", width_hbm, width_ref),
    ]):
        loads[name] = pltpu.make_async_copy(src, dst, load_sem.at[n])
        loads[name].start()

    def remote(src, dst, send, recv, device):
        return pltpu.make_async_remote_copy(
            src_ref=src, dst_ref=dst, send_sem=send, recv_sem=recv, device_id=device, device_id_type=MESH
        )

    def wait_bytes(ref, sem):
        pltpu.make_async_copy(ref, ref, sem).wait()

    loads["k"].wait()
    kall[x_lo] = jnp.concatenate([k_ref[...].astype(f32), jnp.zeros((5, H), f32)], axis=0)
    loads["pos"].wait()
    pos = pos_ref[:, half_atoms]
    pos = jnp.concatenate([pos, jnp.zeros((5, A), f32)], axis=0)
    pos_hi = pos.astype(bf16).astype(f32)
    pos_mid = (pos - pos_hi).astype(bf16).astype(f32)
    pos_low = (pos - pos_hi) - pos_mid
    xmat[...] = jnp.concatenate([pos_hi, pos_mid, pos_low, jnp.zeros((8, A), f32)], axis=0).astype(bf16)
    loads["pad"].wait()
    lanes = lax.broadcasted_iota(jnp.int32, (1, 256), 1)
    for block in range(4):
        mask[:, block * 256 : (block + 1) * 256] = (lanes < pad_ref[x_lo * 4 + block]).astype(f32)

    def trig_half(q):
        kt = kall[q].T
        kcol[pl.ds(pl.multiple_of(q * H, H), H), :] = kt
        kmat[pl.ds(pl.multiple_of(q * H, H), H), :] = jnp.concatenate([kt] * 4, axis=1).astype(bf16)

        def step(i, _):
            rows = pl.ds(pl.multiple_of(q * H + i * 32, 32), 32)
            rows_sin = pl.ds(pl.multiple_of(K + q * H + i * 32, 32), 32)
            left = kmat[rows, :]
            for part_at in range(4):
                cols = slice(part_at * 256, (part_at + 1) * 256)
                cos, sin = sin_cos_turns(dot(left, xmat[:, cols]))
                cos_f[rows, cols] = cos
                sin_f[rows, cols] = sin
                high, low = split(cos)
                t_hi[rows, cols] = high
                t_lo[rows, cols] = low
                high, low = split(sin)
                t_hi[rows_sin, cols] = high
                t_lo[rows_sin, cols] = low
            return 0

        lax.fori_loop(0, H // 32, step, 0)

    low_lanes = lax.broadcasted_iota(jnp.int32, (1, 128), 1) < CH

    def factors(which, q, quant):
        both = quant[...]
        for i in range(2):
            base = q * H + i * 128
            found = []
            for offset in (0, K):
                rows = pl.ds(pl.multiple_of(offset + base, 128), 128)
                one = dot(t_hi[rows, :], both, ((1,), (1,))) + dot(t_lo[rows, :], both, ((1,), (1,)))
                found.append(one + pltpu.roll(one, CH, 1))
            part[which, pl.ds(pl.multiple_of(base, 128), 128), :] = jnp.where(low_lanes, found[0], found[1])

    trig_half(x_lo)

    for name in ("feats", "species", "wq", "embed"):
        loads[name].wait()
    one_hot = (lax.broadcasted_iota(jnp.int32, (16, A), 0) == species_ref[:, half_atoms]).astype(f32)
    q_high, q_low = split(
        mask[...]
        * (
            dot(wq_ref[...], feats[...], ((0,), (0,)), exact)
            + dot(embed_ref[...], one_hot, ((0,), (0,)), exact)
        )
    )
    charge[0:CH, :] = q_high
    charge[CH:128, :] = q_low
    factors(0, x_lo, charge)

    for name in ("grad", "wo", "width"):
        loads[name].wait()
    pl.semaphore_wait(barrier, 39)

    k_copy = remote(kall.at[x_lo], kall.at[x_lo], k_sem.at[0], k_sem.at[1], partner)
    k_copy.start()
    for _, device in y_peers:
        remote(grad_ref, cots.at[y], cot_sem.at[0], cot_sem.at[1], device).start()
    cots[y] = grad_ref[...]

    remote(kall.at[1 - x_lo], kall.at[1 - x_lo], k_sem.at[0], k_sem.at[1], partner).wait_recv()
    trig_half(1 - x_lo)
    factors(0, 1 - x_lo, charge)

    own_rows = pl.ds(pl.multiple_of(core * H, H), H)
    other_rows = pl.ds(pl.multiple_of((1 - core) * H, H), H)

    def pair_sum_copy(which):
        return remote(
            part.at[which, other_rows, :], core_in.at[which],
            core_sem.at[0, which, 0], core_sem.at[1, which, 0], sibling,
        )

    def share_rows(p):
        return pl.ds(pl.multiple_of(p * 8, 8), 8)

    def scatter_start(which):
        pair_sum_copy(which).wait_recv()
        core_sum[which] = part[which, own_rows, :] + core_in[which]
        for p, device in plane_peers:
            remote(
                core_sum.at[which, share_rows(p), :], ring_in.at[which, me],
                plane_sem.at[0, which], plane_sem.at[1, which], device,
            ).start()
        ring_in[which, me] = core_sum[which, share_rows(me), :]

    my_rows = pl.ds(pl.multiple_of(core * H + me * 8, 8), 8)

    def gather_start(which):
        wait_bytes(ring_in.at[which, pl.ds(0, 31)], plane_sem.at[1, which])
        total = ring_in[which, 0]
        for p in range(1, 32):
            total = total + ring_in[which, p]
        wave = two_pi * kcol[my_rows, :]
        square = jnp.sum(wave * wave, axis=1, keepdims=True)
        width = width_ref[...]
        width = jnp.concatenate([width, width], axis=1)
        gain = jnp.exp(-square * width) * 40.0 / (square + 40.0) / 256.0
        owned[which] = gain * total
        for _, device in plane_peers:
            remote(
                owned.at[which], table.at[which, my_rows, :],
                table_sem.at[0, which], table_sem.at[1, which], device,
            ).start()
        table[which, my_rows, :] = owned[which]

    def pair_share_copy(which, rows):
        return remote(
            table.at[which, rows, :], table.at[which, rows, :],
            core_sem.at[0, which, 1], core_sem.at[1, which, 1], sibling,
        )

    def gather_end(which):
        wait_bytes(table.at[which, pl.ds(0, 31 * 8), :], table_sem.at[1, which])
        pair_share_copy(which, own_rows).start()
        pair_share_copy(which, other_rows).wait_recv()

    pair_sum_copy(0).start()
    scatter_start(0)

    wait_bytes(cots.at[pl.ds(0, 7)], cot_sem.at[1])
    for s in range(8):
        cols = slice(s * S, (s + 1) * S)
        high, low = split(mask[:, cols] * dot(wo_ref[...], cots[s], precision=exact))
        adjoint[0:CH, cols] = high
        adjoint[CH:128, cols] = low
    factors(1, 1 - core, adjoint)
    pair_sum_copy(1).start()
    factors(1, core, adjoint)
    scatter_start(1)

    gather_start(0)
    gather_start(1)

    def fields(which):
        high, low = split(table[which].T)
        left = jnp.concatenate(
            [
                jnp.concatenate([high[0:CH], high[CH:128]], axis=1),
                jnp.concatenate([low[0:CH], low[CH:128]], axis=1),
            ],
            axis=0,
        )
        for at in range(4):
            cols = slice(at * 256, (at + 1) * 256)
            both = dot(left, t_hi[:, cols]) + dot(left, t_lo[:, cols])
            field = both[0:CH] + both[CH:128]
            out_y[which, 2 * at] = field[:, 0:S]
            out_y[which, 2 * at + 1] = field[:, S:256]
        for other, device in y_peers:
            remote(
                out_y.at[which, other], in_y.at[which, y], y_sem.at[0, which], y_sem.at[1, which], device
            ).start()
        in_y[which, y] = out_y[which, y]

    def forces(which, quant, add):
        high, low = split(table[which])
        high, low = high.astype(f32), low.astype(f32)
        sin_side = jnp.where(low_lanes, pltpu.roll(high, CH, 1), low).astype(bf16)
        cos_side = jnp.where(low_lanes, high, pltpu.roll(low, CH, 1)).astype(bf16)
        sin_side = jnp.concatenate([sin_side, sin_side], axis=1)
        cos_side = jnp.concatenate([cos_side, cos_side], axis=1)
        columns = [kcol[:, n : n + 1] for n in range(3)]
        for at in range(4):
            cols = slice(at * 256, (at + 1) * 256)
            high_q, low_q = quant[0:CH, cols], quant[CH:128, cols]
            right = jnp.concatenate([high_q, high_q, low_q, low_q], axis=0)
            turn = cos_f[:, cols] * dot(sin_side, right) - sin_f[:, cols] * dot(cos_side, right)
            rows = [jnp.sum(column * turn, axis=0, keepdims=True) for column in columns]
            rows = jnp.concatenate(rows + [jnp.zeros((5, 256), f32)], axis=0)
            for half in range(2):
                slot = 2 * at + half
                here = rows[:, half * S : (half + 1) * S]
                out_f[slot] = out_f[slot] + here if add else here

    gather_end(0)
    fields(0)
    forces(0, adjoint, False)
    gather_end(1)
    fields(1)
    forces(1, charge, True)
    for other, device in y_peers:
        remote(out_f.at[other], in_f.at[y], f_sem.at[0], f_sem.at[1], device).start()
    in_f[y] = out_f[y]

    share = mask[:, pl.ds(pl.multiple_of(y * S, S), S)]

    def collect(which):
        wait_bytes(in_y.at[which, pl.ds(0, 7)], y_sem.at[1, which])
        total = in_y[which, 0]
        for s in range(1, 8):
            total = total + in_y[which, s]
        return share * total

    message_ref[...] = dot(wo_ref[...], collect(0), ((0,), (0,)), exact)
    wait_bytes(in_f.at[pl.ds(0, 7)], f_sem.at[1])
    total = in_f[0]
    for s in range(1, 8):
        total = total + in_f[s]
    force_ref[...] = (two_pi * total)[0:3, :]
    gfeat_ref[...] = dot(wq_ref[...], collect(1), precision=exact)

    k_copy.wait_send()
    wait_bytes(cots.at[pl.ds(0, 7)], cot_sem.at[0])
    for which in range(2):
        pair_sum_copy(which).wait_send()
        pair_share_copy(which, own_rows).wait_send()
        wait_bytes(ring_in.at[which, pl.ds(0, 31)], plane_sem.at[0, which])
        wait_bytes(table.at[which, pl.ds(0, 31 * 8), :], table_sem.at[0, which])
        wait_bytes(in_y.at[which, pl.ds(0, 7)], y_sem.at[0, which])
    wait_bytes(in_f.at[pl.ds(0, 7)], f_sem.at[0])


def on_device(
    positions, feats, species, pad_count, k_lattice, filter_width, w_charge, species_embed, w_out, grad_out
):
    vmem = pl.BlockSpec(memory_space=pltpu.VMEM)
    dma = pltpu.SemaphoreType.DMA
    return pl.pallas_call(
        kernel,
        out_shape=(
            jax.ShapeDtypeStruct((CH, S), f32),
            jax.ShapeDtypeStruct((3, S), f32),
            jax.ShapeDtypeStruct((CH, S), f32),
        ),
        in_specs=[pl.BlockSpec(memory_space=pl.ANY)] * 10,
        out_specs=(vmem, vmem, vmem),
        scratch_shapes=[
            pltpu.VMEM((3, 2 * A), f32),
            pltpu.VMEM((CH, A), f32),
            pltpu.VMEM((1, 2 * A), jnp.int32),
            pltpu.SMEM((8,), jnp.int32),
            pltpu.VMEM((3, H), jnp.int32),
            pltpu.VMEM((1, CH), f32),
            pltpu.VMEM((CH, CH), f32),
            pltpu.VMEM((16, CH), f32),
            pltpu.VMEM((CH, CH), f32),
            pltpu.VMEM((CH, S), f32),
            pltpu.VMEM((2, 8, H), f32),
            pltpu.VMEM((K, 8), f32),
            pltpu.VMEM((K, 32), bf16),
            pltpu.VMEM((32, A), bf16),
            pltpu.VMEM((1, A), f32),
            pltpu.VMEM((2 * K, A), bf16),
            pltpu.VMEM((2 * K, A), bf16),
            pltpu.VMEM((K, A), f32),
            pltpu.VMEM((K, A), f32),
            pltpu.VMEM((128, A), bf16),
            pltpu.VMEM((8, CH, S), f32),
            pltpu.VMEM((128, A), bf16),
            pltpu.VMEM((2, K, 128), f32),
            pltpu.VMEM((2, H, 128), f32),
            pltpu.VMEM((2, H, 128), f32),
            pltpu.VMEM((2, 32, 8, 128), f32),
            pltpu.VMEM((2, 8, 128), f32),
            pltpu.VMEM((2, K, 128), f32),
            pltpu.VMEM((2, 8, CH, S), f32),
            pltpu.VMEM((2, 8, CH, S), f32),
            pltpu.VMEM((8, 8, S), f32),
            pltpu.VMEM((8, 8, S), f32),
            dma((10,)), dma((2,)), dma((2,)), dma((2, 2, 2)),
            dma((2, 2)), dma((2, 2)), dma((2, 2)), dma((2,)),
        ],
        name="ewald",
        compiler_params=pltpu.CompilerParams(
            collective_id=0, has_side_effects=True, vmem_limit_bytes=60 * 1024 * 1024
        ),
    )(
        positions, feats, species.reshape(1, -1), pad_count, k_lattice, filter_width.reshape(1, -1),
        w_charge, species_embed.T, w_out, grad_out,
    )


def solution(mesh):
    placed = (
        P(None, "atoms"),
        P(None, "atoms"),
        P("atoms"),
        P("atoms"),
        P(None, "kvec"),
        P(),
        P(),
        P(),
        P(),
        P(None, ("atoms", "kvec")),
    )
    return jax.shard_map(
        on_device,
        mesh=mesh,
        in_specs=placed,
        out_specs=(P(None, ("atoms", "kvec")),) * 3,
        check_vma=False,
    )
```

```python
import functools
import math

import jax
import jax.numpy as jnp
import numpy as np
from jax import lax
from jax.experimental import pallas as pl
from jax.experimental.pallas import tpu as pltpu
from jax.sharding import PartitionSpec as P

MESH = pl.DeviceIdType.MESH
exact = lax.Precision.HIGHEST
two_pi = 2.0 * math.pi
f32 = jnp.float32
bf16 = jnp.bfloat16

A = 1024
K = 512
H = 256
CH = 64
S = 128


def fit_poly(fn, count, points=2000):
    nodes = 0.25 * (np.cos(np.pi * (np.arange(points) + 0.5) / points) + 1.0) * 0.5
    table = np.vander(nodes / 0.25, count, increasing=True)
    coef = np.linalg.lstsq(table, fn(np.sqrt(nodes)), rcond=None)[0]
    return [float(c) / 0.25**n for n, c in enumerate(coef)]


sin_coef = fit_poly(lambda u: 2.0 * np.sin(np.pi * u) / u, 5)
cos_coef = fit_poly(lambda u: np.cos(np.pi * u), 5)


def horner(coef, sq):
    total = coef[-1]
    for c in coef[-2::-1]:
        total = total * sq + c
    return total


def sin_cos_turns(t):
    u = t - jnp.round(t)
    sq = u * u
    twice_sin = u * horner(sin_coef, sq)
    cos_half = horner(cos_coef, sq)
    return 1.0 - 0.5 * (twice_sin * twice_sin), twice_sin * cos_half


def split(value):
    high = value.astype(bf16)
    return high, (value - high.astype(f32)).astype(bf16)


def dot(a, b, dims=((1,), (0,)), precision=None):
    return lax.dot_general(a, b, (dims, ((), ())), precision=precision, preferred_element_type=f32)


def ring(d, n):
    return min(d, n - d)


y_steps = sorted(range(1, 8), key=lambda d: -ring(d, 8))
plane_steps = sorted(
    [(dx, dz) for dx in range(4) for dz in range(8) if dx or dz],
    key=lambda d: -(ring(d[0], 4) + ring(d[1], 8)),
)
y_order = (0, 1, 7, 2, 6, 3, 5, 4)


def kernel(
    pos_hbm, feats_hbm, species_hbm, pad_hbm, k_hbm, width_hbm, wq_hbm, embed_hbm, wo_hbm, grad_hbm,
    message_ref, force_ref, gfeat_ref,
    pos_ref, feats, species_ref, pad_ref, k_ref, width_ref, wq_ref, embed_ref, wo_ref,
    kall, kcol, kmat, xmat, mask, t_hi, t_lo, e_hi, e_lo, cos_f, sin_f, charge, far_charge, cots, adjoint,
    part_h, part_e, in_h, in_e, sum_h, sum_e, ring_h, ring_e, owned, table, out_y, in_y, out_f, in_f,
    load_sem, k_sem, cot_sem, core_sem, plane_sem, table_sem, share_sem, y_sem, f_sem,
    y_ready, plane_ready, k_ready, core_ready,
):
    atoms_at = lax.axis_index("atoms")
    kvec_at = lax.axis_index("kvec")
    core, z, x_hi = atoms_at % 2, (atoms_at // 2) % 8, atoms_at // 16
    x_lo, y = kvec_at // 8, kvec_at % 8
    x = x_hi * 2 + x_lo
    me = z * 4 + x

    def on_y(other):
        return (atoms_at, x_lo * 8 + other)

    def on_plane(px, pz):
        return ((px // 2) * 16 + pz * 2 + core, (px % 2) * 8 + y)

    def on_place(place):
        return on_plane(place % 4, place // 4)

    y_peers = [((y + d) % 8, on_y((y + d) % 8)) for d in y_steps]
    plane_peers = []
    group_peers = []
    for dx, dz in plane_steps:
        px, pz = (x + dx) % 4, (z + dz) % 8
        plane_peers.append((pz * 4 + px, on_plane(px, pz)))
        if dx % 2 == 0:
            group_peers.append(((px // 2) * 8 + pz, on_plane(px, pz)))
    group_me = x_hi * 8 + z
    sibling = (atoms_at + 1 - 2 * core, kvec_at)
    partner = (atoms_at, (1 - x_lo) * 8 + y)

    def remote(src, dst, send, recv, device):
        return pltpu.make_async_remote_copy(
            src_ref=src, dst_ref=dst, send_sem=send, recv_sem=recv, device_id=device, device_id_type=MESH
        )

    def signal(sem, device):
        pl.semaphore_signal(sem, inc=1, device_id=device, device_id_type=MESH)

    def wait_bytes(ref, sem):
        pltpu.make_async_copy(ref, ref, sem).wait()

    barrier = pltpu.get_barrier_semaphore()
    late = y // 5
    y_rank = (1 - late) * (2 * y - 1) + late * (16 - 2 * y)
    y_before = y_rank + (8 - y) // 8
    for i, other in enumerate(y_order):
        if i:

            @pl.when(i > y_rank)
            def _(other=other):
                signal(barrier, on_y(other))

    lax.fori_loop(me + 1, 32, lambda p, _: (signal(barrier, on_place(p)), 0)[1], 0)

    @pl.when(core == 1)
    def _():
        signal(barrier, sibling)

    loads = {}
    for n, (name, src, dst) in enumerate([
        ("k", k_hbm, k_ref),
        ("pos", pos_hbm, pos_ref),
        ("pad", pad_hbm, pad_ref),
        ("feats", feats_hbm, feats),
        ("species", species_hbm, species_ref),
        ("wq", wq_hbm, wq_ref),
        ("embed", embed_hbm, embed_ref),
        ("wo", wo_hbm, wo_ref),
        ("width", width_hbm, width_ref),
        ("grad", grad_hbm, cots.at[y]),
    ]):
        loads[name] = pltpu.make_async_copy(src, dst, load_sem.at[n])
        loads[name].start()

    before = y_before + me + 1 - core

    @pl.when(before > 0)
    def _():
        pl.semaphore_wait(barrier, before)

    for i, other in enumerate(y_order[:-1]):

        @pl.when(i < y_rank)
        def _(other=other):
            signal(y_ready.at[y], on_y(other))

    @pl.when(x_lo == 1)
    def _():
        signal(k_ready, partner)

    def cot_copy(device):
        return remote(grad_hbm, cots.at[y], cot_sem.at[0], cot_sem.at[1], device)

    for i, other in enumerate(y_order[:-1]):

        @pl.when(i < y_rank)
        def _(other=other):
            cot_copy(on_y(other)).start()

    @pl.when(core == 0)
    def _():
        signal(core_ready, sibling)

    loads["k"].wait()
    kall[x_lo] = jnp.concatenate([k_ref[...].astype(f32), jnp.zeros((5, H), f32)], axis=0)
    k_copy = remote(kall.at[x_lo], kall.at[x_lo], k_sem.at[0], k_sem.at[1], partner)

    @pl.when(x_lo == 1)
    def _():
        k_copy.start()

    lax.fori_loop(0, me, lambda p, _: (signal(plane_ready, on_place(p)), 0)[1], 0)

    halves = [pl.ds(pl.multiple_of(h * A, A), A) for h in (x_lo, 1 - x_lo)]
    loads["pos"].wait()
    loads["pad"].wait()
    lanes = lax.broadcasted_iota(jnp.int32, (1, 256), 1)
    for n, h in enumerate((x_lo, 1 - x_lo)):
        pos = jnp.concatenate([pos_ref[:, halves[n]], jnp.zeros((5, A), f32)], axis=0)
        pos_hi = pos.astype(bf16).astype(f32)
        pos_mid = (pos - pos_hi).astype(bf16).astype(f32)
        pos_low = (pos - pos_hi) - pos_mid
        xmat[n] = jnp.concatenate([pos_hi, pos_mid, pos_low, jnp.zeros((8, A), f32)], axis=0).astype(bf16)
        for block in range(4):
            mask[n, :, block * 256 : (block + 1) * 256] = (lanes < pad_ref[h * 4 + block]).astype(f32)

    def set_k(q):
        kt = kall[q].T
        kcol[pl.ds(pl.multiple_of(q * H, H), H), :] = kt
        kmat[pl.ds(pl.multiple_of(q * H, H), H), :] = jnp.concatenate([kt] * 4, axis=1).astype(bf16)

    def trig(q, n, high_ref, low_ref, cos_base, sin_base, keep):
        def step(i, _):
            rows = pl.ds(pl.multiple_of(q * H + i * 32, 32), 32)
            cos_rows = pl.ds(pl.multiple_of(cos_base + i * 32, 32), 32)
            sin_rows = pl.ds(pl.multiple_of(sin_base + i * 32, 32), 32)
            left = kmat[rows, :]
            for at in range(4):
                cols = slice(at * 256, (at + 1) * 256)
                cos, sin = sin_cos_turns(dot(left, xmat[n, :, cols]))
                if keep:
                    cos_f[rows, cols] = cos
                    sin_f[rows, cols] = sin
                high_ref[cos_rows, cols], low_ref[cos_rows, cols] = split(cos)
                high_ref[sin_rows, cols], low_ref[sin_rows, cols] = split(sin)
            return 0

        lax.fori_loop(0, H // 32, step, 0)

    low_lanes = lax.broadcasted_iota(jnp.int32, (1, 128), 1) < CH

    def factors(out_ref, base, terms):
        for i in range(2):
            found = []
            for sine in (0, 1):
                one = jnp.zeros((128, 128), f32)
                for high_ref, low_ref, cos_base, sin_base, quant in terms:
                    rows = pl.ds(pl.multiple_of((sin_base if sine else cos_base) + i * 128, 128), 128)
                    one = one + dot(high_ref[rows, :], quant[...], ((1,), (1,)))
                    one = one + dot(low_ref[rows, :], quant[...], ((1,), (1,)))
                found.append(one + pltpu.roll(one, CH, 1))
            out_ref[pl.ds(pl.multiple_of(base + i * 128, 128), 128), :] = jnp.where(low_lanes, found[0], found[1])

    set_k(x_lo)
    trig(x_lo, 0, t_hi, t_lo, x_lo * H, K + x_lo * H, True)

    for name in ("feats", "species", "wq", "embed"):
        loads[name].wait()
    for n, quant in enumerate((charge, far_charge)):
        one_hot = (lax.broadcasted_iota(jnp.int32, (16, A), 0) == species_ref[:, halves[n]]).astype(f32)
        quant[0:CH, :], quant[CH:128, :] = split(
            mask[n]
            * (
                dot(wq_ref[...], feats[:, halves[n]], ((0,), (0,)), exact)
                + dot(embed_ref[...], one_hot, ((0,), (0,)), exact)
            )
        )

    @pl.when(x_lo == 0)
    def _():
        pl.semaphore_wait(k_ready, 1)
        k_copy.start()

    trig(x_lo, 1, e_hi, e_lo, 0, H, False)
    factors(
        part_h, 0, [(t_hi, t_lo, x_lo * H, K + x_lo * H, charge), (e_hi, e_lo, 0, H, far_charge)]
    )

    h_pair = remote(part_h, in_h, core_sem.at[0], core_sem.at[1], sibling)

    @pl.when(core == 1)
    def _():
        pl.semaphore_wait(core_ready, 1)
        h_pair.start()

    for i, other in enumerate(y_order):
        if i:

            @pl.when(i > y_rank)
            def _(other=other):
                pl.semaphore_wait(y_ready.at[other], 1)
                cot_copy(on_y(other)).start()

    remote(kall.at[1 - x_lo], kall.at[1 - x_lo], k_sem.at[0], k_sem.at[1], partner).wait_recv()
    set_k(1 - x_lo)
    trig(1 - x_lo, 0, t_hi, t_lo, (1 - x_lo) * H, K + (1 - x_lo) * H, True)

    def gain_of(first):
        wave = two_pi * kcol[pl.ds(pl.multiple_of(first, 16), 16), :]
        square = jnp.sum(wave * wave, axis=1, keepdims=True)
        width = width_ref[...]
        width = jnp.concatenate([width, width], axis=1)
        return jnp.exp(-square * width) * 40.0 / (square + 40.0) / 256.0

    def scatter(total, peers, ring_ref, mine):
        for p, device in peers:
            remote(
                total.at[pl.ds(pl.multiple_of(p * 16, 16), 16), :], ring_ref.at[mine],
                plane_sem.at[0], plane_sem.at[1], device,
            ).start()
        ring_ref[mine] = total[pl.ds(pl.multiple_of(mine * 16, 16), 16), :]

    def gather(which, first, ring_ref, count):
        wait_bytes(ring_ref.at[pl.ds(0, count - 1)], plane_sem.at[1])
        total = ring_ref[0]
        for p in range(1, count):
            total = total + ring_ref[p]
        owned[...] = gain_of(first) * total
        rows = pl.ds(pl.multiple_of(first, 16), 16)
        for _, device in plane_peers:
            remote(owned, table.at[which, rows, :], table_sem.at[0], table_sem.at[1], device).start()
        table[which, rows, :] = owned[...]

    def share_copy(which):
        return remote(table.at[which], table.at[which], share_sem.at[0], share_sem.at[1], sibling)

    def share(which):
        wait_bytes(table.at[which, pl.ds(0, 31 * 16), :], table_sem.at[1])
        share_copy(which).start()

    @pl.when(me < 31)
    def _():
        pl.semaphore_wait(plane_ready, 31 - me)

    @pl.when(core == 0)
    def _():
        h_pair.wait_recv()
        sum_h[...] = part_h[...] + in_h[...]
        scatter(sum_h, group_peers, ring_h, group_me)

    for name in ("wo", "width", "grad"):
        loads[name].wait()
    wait_bytes(cots.at[pl.ds(0, 7)], cot_sem.at[1])
    for s in range(8):
        cols = slice(s * S, (s + 1) * S)
        adjoint[0:CH, cols], adjoint[CH:128, cols] = split(
            mask[0, :, cols] * dot(wo_ref[...], cots[s], precision=exact)
        )

    def e_pair(q):
        rows = pl.ds(q * H, H)
        return remote(part_e.at[rows, :], in_e.at[rows, :], core_sem.at[0], core_sem.at[1], sibling)

    for q in range(2):
        factors(part_e, q * H, [(t_hi, t_lo, q * H, K + q * H, adjoint)])

        @pl.when(core == 0)
        def _(q=q):
            e_pair(q).start()

    @pl.when(core == 1)
    def _():
        wait_bytes(in_e, core_sem.at[1])
        sum_e[...] = part_e[...] + in_e[...]
        scatter(sum_e, plane_peers, ring_e, me)

    @pl.when(core == 0)
    def _():
        gather(0, x_lo * H + group_me * 16, ring_h, 16)

    @pl.when(core == 1)
    def _():
        gather(1, me * 16, ring_e, 32)

    def fields(which):
        high, low = split(table[which].T)
        left = jnp.concatenate(
            [
                jnp.concatenate([high[0:CH], high[CH:128]], axis=1),
                jnp.concatenate([low[0:CH], low[CH:128]], axis=1),
            ],
            axis=0,
        )
        for at in range(4):
            cols = slice(at * 256, (at + 1) * 256)
            both = dot(left, t_hi[:, cols]) + dot(left, t_lo[:, cols])
            field = both[0:CH] + both[CH:128]
            out_y[which, 2 * at] = field[:, 0:S]
            out_y[which, 2 * at + 1] = field[:, S:256]
        for other, device in y_peers:
            remote(
                out_y.at[which, other], in_y.at[which, y], y_sem.at[0, which], y_sem.at[1, which], device
            ).start()
        in_y[which, y] = out_y[which, y]

    def forces(which, quant, add):
        high, low = split(table[which])
        high, low = high.astype(f32), low.astype(f32)
        sin_side = jnp.where(low_lanes, pltpu.roll(high, CH, 1), low).astype(bf16)
        cos_side = jnp.where(low_lanes, high, pltpu.roll(low, CH, 1)).astype(bf16)
        sin_side = jnp.concatenate([sin_side, sin_side], axis=1)
        cos_side = jnp.concatenate([cos_side, cos_side], axis=1)
        columns = [kcol[:, n : n + 1] for n in range(3)]
        for at in range(4):
            cols = slice(at * 256, (at + 1) * 256)
            high_q, low_q = quant[0:CH, cols], quant[CH:128, cols]
            right = jnp.concatenate([high_q, high_q, low_q, low_q], axis=0)
            turn = cos_f[:, cols] * dot(sin_side, right) - sin_f[:, cols] * dot(cos_side, right)
            rows = [jnp.sum(column * turn, axis=0, keepdims=True) for column in columns]
            rows = jnp.concatenate(rows + [jnp.zeros((5, 256), f32)], axis=0)
            for half in range(2):
                slot = 2 * at + half
                here = rows[:, half * S : (half + 1) * S]
                out_f[slot] = out_f[slot] + here if add else here

    @pl.when(core == 0)
    def _():
        share(0)

    @pl.when(core == 1)
    def _():
        share_copy(0).wait_recv()

    fields(0)
    forces(0, adjoint, False)

    @pl.when(core == 1)
    def _():
        share(1)

    @pl.when(core == 0)
    def _():
        share_copy(1).wait_recv()

    fields(1)
    forces(1, charge, True)
    for other, device in y_peers:
        remote(out_f.at[other], in_f.at[y], f_sem.at[0], f_sem.at[1], device).start()
    in_f[y] = out_f[y]

    mine = mask[0, :, pl.ds(pl.multiple_of(y * S, S), S)]

    def collect(which):
        wait_bytes(in_y.at[which, pl.ds(0, 7)], y_sem.at[1, which])
        total = in_y[which, 0]
        for s in range(1, 8):
            total = total + in_y[which, s]
        return mine * total

    message_ref[...] = dot(wo_ref[...], collect(0), ((0,), (0,)), exact)
    wait_bytes(in_f.at[pl.ds(0, 7)], f_sem.at[1])
    total = in_f[0]
    for s in range(1, 8):
        total = total + in_f[s]
    force_ref[...] = (two_pi * total)[0:3, :]
    gfeat_ref[...] = dot(wq_ref[...], collect(1), precision=exact)

    k_copy.wait_send()
    wait_bytes(cots.at[pl.ds(0, 7)], cot_sem.at[0])

    @pl.when(core == 0)
    def _():
        wait_bytes(in_e, core_sem.at[0])
        wait_bytes(ring_h.at[pl.ds(0, 15)], plane_sem.at[0])
        share_copy(0).wait_send()

    @pl.when(core == 1)
    def _():
        h_pair.wait_send()
        wait_bytes(ring_e.at[pl.ds(0, 31)], plane_sem.at[0])
        share_copy(1).wait_send()

    wait_bytes(table.at[0, pl.ds(0, 31 * 16), :], table_sem.at[0])
    for which in range(2):
        wait_bytes(in_y.at[which, pl.ds(0, 7)], y_sem.at[0, which])
    wait_bytes(in_f.at[pl.ds(0, 7)], f_sem.at[0])


def on_device(
    positions, feats, species, pad_count, k_lattice, filter_width, w_charge, species_embed, w_out, grad_out
):
    vmem = pl.BlockSpec(memory_space=pltpu.VMEM)
    dma = pltpu.SemaphoreType.DMA
    regular = pltpu.SemaphoreType.REGULAR
    return pl.pallas_call(
        kernel,
        out_shape=(
            jax.ShapeDtypeStruct((CH, S), f32),
            jax.ShapeDtypeStruct((3, S), f32),
            jax.ShapeDtypeStruct((CH, S), f32),
        ),
        in_specs=[pl.BlockSpec(memory_space=pl.ANY)] * 10,
        out_specs=(vmem, vmem, vmem),
        scratch_shapes=[
            pltpu.VMEM((3, 2 * A), f32),
            pltpu.VMEM((CH, 2 * A), f32),
            pltpu.VMEM((1, 2 * A), jnp.int32),
            pltpu.SMEM((8,), jnp.int32),
            pltpu.VMEM((3, H), jnp.int32),
            pltpu.VMEM((1, CH), f32),
            pltpu.VMEM((CH, CH), f32),
            pltpu.VMEM((16, CH), f32),
            pltpu.VMEM((CH, CH), f32),
            pltpu.VMEM((2, 8, H), f32),
            pltpu.VMEM((K, 8), f32),
            pltpu.VMEM((K, 32), bf16),
            pltpu.VMEM((2, 32, A), bf16),
            pltpu.VMEM((2, 1, A), f32),
            pltpu.VMEM((2 * K, A), bf16),
            pltpu.VMEM((2 * K, A), bf16),
            pltpu.VMEM((2 * H, A), bf16),
            pltpu.VMEM((2 * H, A), bf16),
            pltpu.VMEM((K, A), f32),
            pltpu.VMEM((K, A), f32),
            pltpu.VMEM((128, A), bf16),
            pltpu.VMEM((128, A), bf16),
            pltpu.VMEM((8, CH, S), f32),
            pltpu.VMEM((128, A), bf16),
            pltpu.VMEM((H, 128), f32),
            pltpu.VMEM((K, 128), f32),
            pltpu.VMEM((H, 128), f32),
            pltpu.VMEM((K, 128), f32),
            pltpu.VMEM((H, 128), f32),
            pltpu.VMEM((K, 128), f32),
            pltpu.VMEM((16, 16, 128), f32),
            pltpu.VMEM((32, 16, 128), f32),
            pltpu.VMEM((16, 128), f32),
            pltpu.VMEM((2, K, 128), f32),
            pltpu.VMEM((2, 8, CH, S), f32),
            pltpu.VMEM((2, 8, CH, S), f32),
            pltpu.VMEM((8, 8, S), f32),
            pltpu.VMEM((8, 8, S), f32),
            dma((10,)), dma((2,)), dma((2,)), dma((2,)),
            dma((2,)), dma((2,)), dma((2,)), dma((2, 2)), dma((2,)),
            regular((8,)), regular, regular, regular,
        ],
        name="ewald",
        compiler_params=pltpu.CompilerParams(
            collective_id=0, has_side_effects=True, vmem_limit_bytes=60 * 1024 * 1024
        ),
    )(
        positions, feats, species.reshape(1, -1), pad_count, k_lattice, filter_width.reshape(1, -1),
        w_charge, species_embed.T, w_out, grad_out,
    )


def solution(mesh):
    placed = (
        P(None, "atoms"),
        P(None, "atoms"),
        P("atoms"),
        P("atoms"),
        P(None, "kvec"),
        P(),
        P(),
        P(),
        P(),
        P(None, ("atoms", "kvec")),
    )
    return jax.shard_map(
        on_device,
        mesh=mesh,
        in_specs=placed,
        out_specs=(P(None, ("atoms", "kvec")),) * 3,
        check_vma=False,
    )
```

```python
import functools
import math

import jax
import jax.numpy as jnp
import numpy as np
from jax import lax
from jax.experimental import pallas as pl
from jax.experimental.pallas import tpu as pltpu
from jax.sharding import PartitionSpec as P

MESH = pl.DeviceIdType.MESH
exact = lax.Precision.HIGHEST
two_pi = 2.0 * math.pi
f32 = jnp.float32
bf16 = jnp.bfloat16

A = 1024
K = 512
H = 256
CH = 64
S = 128


def fit_poly(fn, count, points=2000):
    nodes = 0.25 * (np.cos(np.pi * (np.arange(points) + 0.5) / points) + 1.0) * 0.5
    table = np.vander(nodes / 0.25, count, increasing=True)
    coef = np.linalg.lstsq(table, fn(np.sqrt(nodes)), rcond=None)[0]
    return [float(c) / 0.25**n for n, c in enumerate(coef)]


sin_coef = fit_poly(lambda u: 2.0 * np.sin(np.pi * u) / u, 5)
cos_coef = fit_poly(lambda u: np.cos(np.pi * u), 5)


def horner(coef, sq):
    total = coef[-1]
    for c in coef[-2::-1]:
        total = total * sq + c
    return total


def sin_cos_turns(t):
    u = t - jnp.round(t)
    sq = u * u
    twice_sin = u * horner(sin_coef, sq)
    cos_half = horner(cos_coef, sq)
    return 1.0 - 0.5 * (twice_sin * twice_sin), twice_sin * cos_half


def split(value):
    high = value.astype(bf16)
    return high, (value - high.astype(f32)).astype(bf16)


def dot(a, b, dims=((1,), (0,)), precision=None):
    return lax.dot_general(a, b, (dims, ((), ())), precision=precision, preferred_element_type=f32)


def ring(d, n):
    return min(d, n - d)


y_steps = sorted(range(1, 8), key=lambda d: -ring(d, 8))
plane_steps = sorted(
    [(dx, dz) for dx in range(4) for dz in range(8) if dx or dz],
    key=lambda d: -(ring(d[0], 4) + ring(d[1], 8)),
)
plane_far = [int(ring(dz, 8) > 2) for _, dz in plane_steps]
y_order = (0, 1, 7, 2, 6, 3, 5, 4)


def kernel(
    pos_hbm, feats_hbm, species_hbm, pad_hbm, k_hbm, width_hbm, wq_hbm, embed_hbm, wo_hbm, grad_hbm,
    message_ref, force_ref, gfeat_ref,
    pos_ref, feats, species_ref, pad_ref, k_ref, width_ref, wq_ref, embed_ref, wo_ref,
    kall, kcol, kmat, xmat, mask, t_hi, t_lo, e_hi, e_lo, cos_f, sin_f, charge, far_charge, cots, adjoint,
    part_h, part_e, in_h, in_e, sum_h, sum_e, ring_h, ring_e, owned, table, out_y, in_y, out_f, in_f,
    load_sem, k_sem, cot_sem, core_sem, plane_sem, table_sem, share_sem, y_sem, f_sem,
    y_ready, plane_ready, k_ready, core_ready,
):
    atoms_at = lax.axis_index("atoms")
    kvec_at = lax.axis_index("kvec")
    core, z, x_hi = atoms_at % 2, (atoms_at // 2) % 8, atoms_at // 16
    x_lo, y = kvec_at // 8, kvec_at % 8
    x = x_hi * 2 + x_lo
    me = z * 4 + x
    group_me = x_hi * 8 + z
    x_at = x_lo * 2 + x_hi
    place = x_at * 8 + z

    def on_y(other):
        return (atoms_at, x_lo * 8 + other)

    def on_plane(px, pz):
        return ((px // 2) * 16 + pz * 2 + core, (px % 2) * 8 + y)

    def on_start(p):
        return on_plane(p % 4, p // 4)

    y_peers = [((y + d) % 8, on_y((y + d) % 8)) for d in y_steps]
    plane_peers = []
    group_peers = []
    for dx, dz in plane_steps:
        px, pz = (x + dx) % 4, (z + dz) % 8
        plane_peers.append((((px % 2) * 2 + px // 2) * 8 + pz, on_plane(px, pz)))
        if dx % 2 == 0:
            group_peers.append(((px // 2) * 8 + pz, on_plane(px, pz)))
    sibling = (atoms_at + 1 - 2 * core, kvec_at)
    partner = (atoms_at, (1 - x_lo) * 8 + y)

    def remote(src, dst, send, recv, device):
        return pltpu.make_async_remote_copy(
            src_ref=src, dst_ref=dst, send_sem=send, recv_sem=recv, device_id=device, device_id_type=MESH
        )

    def signal(sem, device):
        pl.semaphore_signal(sem, inc=1, device_id=device, device_id_type=MESH)

    def wait_bytes(ref, sem):
        pltpu.make_async_copy(ref, ref, sem).wait()

    barrier = pltpu.get_barrier_semaphore()
    late = y // 5
    y_rank = (1 - late) * (2 * y - 1) + late * (16 - 2 * y)
    y_before = y_rank + (8 - y) // 8
    for i, other in enumerate(y_order):
        if i:

            @pl.when(i > y_rank)
            def _(other=other):
                signal(barrier, on_y(other))

    lax.fori_loop(me + 1, 32, lambda p, _: (signal(barrier, on_start(p)), 0)[1], 0)

    @pl.when(core == 1)
    def _():
        signal(barrier, sibling)

    loads = {}
    for n, (name, src, dst) in enumerate([
        ("k", k_hbm, k_ref),
        ("pos", pos_hbm, pos_ref),
        ("pad", pad_hbm, pad_ref),
        ("feats", feats_hbm, feats),
        ("species", species_hbm, species_ref),
        ("wq", wq_hbm, wq_ref),
        ("embed", embed_hbm, embed_ref),
        ("wo", wo_hbm, wo_ref),
        ("width", width_hbm, width_ref),
        ("grad", grad_hbm, cots.at[y]),
    ]):
        loads[name] = pltpu.make_async_copy(src, dst, load_sem.at[n])
        loads[name].start()

    before = y_before + me + 1 - core

    @pl.when(before > 0)
    def _():
        pl.semaphore_wait(barrier, before)

    for i, other in enumerate(y_order[:-1]):

        @pl.when(i < y_rank)
        def _(other=other):
            signal(y_ready.at[y], on_y(other))

    @pl.when(x_lo == 1)
    def _():
        signal(k_ready, partner)

    def cot_copy(device):
        return remote(grad_hbm, cots.at[y], cot_sem.at[0], cot_sem.at[1], device)

    for i, other in enumerate(y_order[:-1]):

        @pl.when(i < y_rank)
        def _(other=other):
            cot_copy(on_y(other)).start()

    @pl.when(core == 0)
    def _():
        signal(core_ready, sibling)

    loads["k"].wait()
    kall[x_lo] = jnp.concatenate([k_ref[...].astype(f32), jnp.zeros((5, H), f32)], axis=0)
    k_copy = remote(kall.at[x_lo], kall.at[x_lo], k_sem.at[0], k_sem.at[1], partner)

    @pl.when(x_lo == 1)
    def _():
        k_copy.start()

    lax.fori_loop(0, me, lambda p, _: (signal(plane_ready, on_start(p)), 0)[1], 0)

    halves = [pl.ds(pl.multiple_of(h * A, A), A) for h in (x_lo, 1 - x_lo)]
    loads["pos"].wait()
    loads["pad"].wait()
    lanes = lax.broadcasted_iota(jnp.int32, (1, 256), 1)
    for n, h in enumerate((x_lo, 1 - x_lo)):
        pos = jnp.concatenate([pos_ref[:, halves[n]], jnp.zeros((5, A), f32)], axis=0)
        pos_hi = pos.astype(bf16).astype(f32)
        pos_mid = (pos - pos_hi).astype(bf16).astype(f32)
        pos_low = (pos - pos_hi) - pos_mid
        xmat[n] = jnp.concatenate([pos_hi, pos_mid, pos_low, jnp.zeros((8, A), f32)], axis=0).astype(bf16)
        for block in range(4):
            mask[n, :, block * 256 : (block + 1) * 256] = (lanes < pad_ref[h * 4 + block]).astype(f32)

    def set_k(q):
        kt = kall[q].T
        kcol[pl.ds(pl.multiple_of(q * H, H), H), :] = kt
        kmat[pl.ds(pl.multiple_of(q * H, H), H), :] = jnp.concatenate([kt] * 4, axis=1).astype(bf16)

    def trig(q, n, high_ref, low_ref, cos_base, sin_base, keep):
        def step(i, _):
            rows = pl.ds(pl.multiple_of(q * H + i * 32, 32), 32)
            cos_rows = pl.ds(pl.multiple_of(cos_base + i * 32, 32), 32)
            sin_rows = pl.ds(pl.multiple_of(sin_base + i * 32, 32), 32)
            left = kmat[rows, :]
            for at in range(4):
                cols = slice(at * 256, (at + 1) * 256)
                cos, sin = sin_cos_turns(dot(left, xmat[n, :, cols]))
                if keep:
                    cos_f[rows, cols] = cos
                    sin_f[rows, cols] = sin
                high_ref[cos_rows, cols], low_ref[cos_rows, cols] = split(cos)
                high_ref[sin_rows, cols], low_ref[sin_rows, cols] = split(sin)
            return 0

        lax.fori_loop(0, H // 32, step, 0)

    low_lanes = lax.broadcasted_iota(jnp.int32, (1, 128), 1) < CH

    def factors(out_ref, base, terms):
        for i in range(2):
            found = []
            for sine in (0, 1):
                one = jnp.zeros((128, 128), f32)
                for high_ref, low_ref, cos_base, sin_base, quant in terms:
                    rows = pl.ds(pl.multiple_of((sin_base if sine else cos_base) + i * 128, 128), 128)
                    one = one + dot(high_ref[rows, :], quant[...], ((1,), (1,)))
                    one = one + dot(low_ref[rows, :], quant[...], ((1,), (1,)))
                found.append(one + pltpu.roll(one, CH, 1))
            out_ref[pl.ds(pl.multiple_of(base + i * 128, 128), 128), :] = jnp.where(low_lanes, found[0], found[1])

    set_k(x_lo)
    trig(x_lo, 0, t_hi, t_lo, x_lo * H, K + x_lo * H, True)

    @pl.when(x_lo == 0)
    def _():
        pl.semaphore_wait(k_ready, 1)
        k_copy.start()

    for i, other in enumerate(y_order):
        if i:

            @pl.when(i > y_rank)
            def _(other=other):
                pl.semaphore_wait(y_ready.at[other], 1)
                cot_copy(on_y(other)).start()

    for name in ("feats", "species", "wq", "embed"):
        loads[name].wait()
    for n, quant in enumerate((charge, far_charge)):
        one_hot = (lax.broadcasted_iota(jnp.int32, (16, A), 0) == species_ref[:, halves[n]]).astype(f32)
        quant[0:CH, :], quant[CH:128, :] = split(
            mask[n]
            * (
                dot(wq_ref[...], feats[:, halves[n]], ((0,), (0,)), exact)
                + dot(embed_ref[...], one_hot, ((0,), (0,)), exact)
            )
        )

    trig(x_lo, 1, e_hi, e_lo, 0, H, False)
    factors(
        part_h, 0, [(t_hi, t_lo, x_lo * H, K + x_lo * H, charge), (e_hi, e_lo, 0, H, far_charge)]
    )

    h_pair = remote(part_h, in_h, core_sem.at[0], core_sem.at[1], sibling)

    @pl.when(core == 1)
    def _():
        pl.semaphore_wait(core_ready, 1)
        h_pair.start()

    remote(kall.at[1 - x_lo], kall.at[1 - x_lo], k_sem.at[0], k_sem.at[1], partner).wait_recv()
    set_k(1 - x_lo)
    trig(1 - x_lo, 0, t_hi, t_lo, (1 - x_lo) * H, K + (1 - x_lo) * H, True)

    def gain_of(first):
        wave = two_pi * kcol[pl.ds(pl.multiple_of(first, 16), 16), :]
        square = jnp.sum(wave * wave, axis=1, keepdims=True)
        width = width_ref[...]
        width = jnp.concatenate([width, width], axis=1)
        return jnp.exp(-square * width) * 40.0 / (square + 40.0) / 256.0

    def scatter(total, peers, ring_ref, mine):
        for p, device in peers:
            remote(
                total.at[pl.ds(pl.multiple_of(p * 16, 16), 16), :], ring_ref.at[mine],
                plane_sem.at[0], plane_sem.at[1], device,
            ).start()
        ring_ref[mine] = total[pl.ds(pl.multiple_of(mine * 16, 16), 16), :]

    def gather(which, ring_ref, count):
        wait_bytes(ring_ref.at[pl.ds(0, count - 1)], plane_sem.at[1])
        total = ring_ref[0]
        for p in range(1, count):
            total = total + ring_ref[p]
        owned[...] = gain_of(place * 16) * total
        for (_, device), far in zip(plane_peers, plane_far):
            remote(owned, table.at[which, x_at, z], table_sem.at[0], table_sem.at[1 + far], device).start()
        table[which, x_at, z] = owned[...]

    def share(which):
        for far, steps in enumerate(((0, 1, 7, 2, 6), (3, 5, 4))):
            wait_bytes(ring_e.at[pl.ds(0, 4 * len(steps) - (1 - far))], table_sem.at[1 + far])
            for step in steps:
                rows = table.at[which, :, (z + step) % 8]
                remote(rows, rows, share_sem.at[0], share_sem.at[1], sibling).start()

    @pl.when(me < 31)
    def _():
        pl.semaphore_wait(plane_ready, 31 - me)

    @pl.when(core == 0)
    def _():
        h_pair.wait_recv()
        sum_h[...] = part_h[...] + in_h[...]
        scatter(sum_h, group_peers, ring_h, group_me)

    for name in ("wo", "width", "grad"):
        loads[name].wait()
    wait_bytes(cots.at[pl.ds(0, 7)], cot_sem.at[1])
    for s in range(8):
        cols = slice(s * S, (s + 1) * S)
        adjoint[0:CH, cols], adjoint[CH:128, cols] = split(
            mask[0, :, cols] * dot(wo_ref[...], cots[s], precision=exact)
        )

    def e_pair(q):
        rows = pl.ds(q * H, H)
        return remote(part_e.at[rows, :], in_e.at[rows, :], core_sem.at[0], core_sem.at[1], sibling)

    for q in range(2):
        factors(part_e, q * H, [(t_hi, t_lo, q * H, K + q * H, adjoint)])

        @pl.when(core == 0)
        def _(q=q):
            e_pair(q).start()

    @pl.when(core == 1)
    def _():
        wait_bytes(in_e, core_sem.at[1])
        sum_e[...] = part_e[...] + in_e[...]
        scatter(sum_e, plane_peers, ring_e, place)

    @pl.when(core == 0)
    def _():
        gather(0, ring_h, 16)

    @pl.when(core == 1)
    def _():
        gather(1, ring_e, 32)

    def y_copy(which, other):
        return remote(
            out_y.at[which, other], in_y.at[which, y], y_sem.at[0, which], y_sem.at[1, which], on_y(other)
        )

    def fields(which):
        high, low = split(table[which].reshape(K, 128).T)
        left = jnp.concatenate(
            [
                jnp.concatenate([high[0:CH], high[CH:128]], axis=1),
                jnp.concatenate([low[0:CH], low[CH:128]], axis=1),
            ],
            axis=0,
        )
        for turn in (2, 1, 3, 0):
            at = (y // 2 + turn) % 4
            cols = pl.ds(pl.multiple_of(at * 256, 256), 256)
            both = dot(left, t_hi[:, cols]) + dot(left, t_lo[:, cols])
            field = both[0:CH] + both[CH:128]
            for n in range(2):
                other = 2 * at + n
                out_y[which, other] = field[:, n * S : (n + 1) * S]
                if turn:
                    y_copy(which, other).start()
                else:

                    @pl.when(other != y)
                    def _(other=other):
                        y_copy(which, other).start()

        in_y[which, y] = out_y[which, y]

    def forces(which, quant, add):
        high, low = split(table[which].reshape(K, 128))
        high, low = high.astype(f32), low.astype(f32)
        sin_side = jnp.where(low_lanes, pltpu.roll(high, CH, 1), low).astype(bf16)
        cos_side = jnp.where(low_lanes, high, pltpu.roll(low, CH, 1)).astype(bf16)
        sin_side = jnp.concatenate([sin_side, sin_side], axis=1)
        cos_side = jnp.concatenate([cos_side, cos_side], axis=1)
        columns = [kcol[:, n : n + 1] for n in range(3)]
        for at in range(4):
            cols = slice(at * 256, (at + 1) * 256)
            high_q, low_q = quant[0:CH, cols], quant[CH:128, cols]
            right = jnp.concatenate([high_q, high_q, low_q, low_q], axis=0)
            turn = cos_f[:, cols] * dot(sin_side, right) - sin_f[:, cols] * dot(cos_side, right)
            rows = [jnp.sum(column * turn, axis=0, keepdims=True) for column in columns]
            rows = jnp.concatenate(rows + [jnp.zeros((5, 256), f32)], axis=0)
            for half in range(2):
                slot = 2 * at + half
                here = rows[:, half * S : (half + 1) * S]
                out_f[slot] = out_f[slot] + here if add else here

    @pl.when(core == 0)
    def _():
        share(0)

    @pl.when(core == 1)
    def _():
        wait_bytes(table.at[0], share_sem.at[1])

    fields(0)
    forces(0, adjoint, False)

    @pl.when(core == 1)
    def _():
        share(1)

    @pl.when(core == 0)
    def _():
        wait_bytes(table.at[1], share_sem.at[1])

    fields(1)
    forces(1, charge, True)
    for other, device in y_peers:
        remote(out_f.at[other], in_f.at[y], f_sem.at[0], f_sem.at[1], device).start()
    in_f[y] = out_f[y]

    mine = mask[0, :, pl.ds(pl.multiple_of(y * S, S), S)]

    def collect(which):
        wait_bytes(in_y.at[which, pl.ds(0, 7)], y_sem.at[1, which])
        total = in_y[which, 0]
        for s in range(1, 8):
            total = total + in_y[which, s]
        return mine * total

    message_ref[...] = dot(wo_ref[...], collect(0), ((0,), (0,)), exact)
    wait_bytes(in_f.at[pl.ds(0, 7)], f_sem.at[1])
    total = in_f[0]
    for s in range(1, 8):
        total = total + in_f[s]
    force_ref[...] = (two_pi * total)[0:3, :]
    gfeat_ref[...] = dot(wq_ref[...], collect(1), precision=exact)

    k_copy.wait_send()
    wait_bytes(cots.at[pl.ds(0, 7)], cot_sem.at[0])

    @pl.when(core == 0)
    def _():
        wait_bytes(in_e, core_sem.at[0])
        wait_bytes(ring_h.at[pl.ds(0, 15)], plane_sem.at[0])
        wait_bytes(table.at[0], share_sem.at[0])

    @pl.when(core == 1)
    def _():
        h_pair.wait_send()
        wait_bytes(ring_e.at[pl.ds(0, 31)], plane_sem.at[0])
        wait_bytes(table.at[1], share_sem.at[0])

    wait_bytes(ring_e.at[pl.ds(0, 31)], table_sem.at[0])
    for which in range(2):
        wait_bytes(in_y.at[which, pl.ds(0, 7)], y_sem.at[0, which])
    wait_bytes(in_f.at[pl.ds(0, 7)], f_sem.at[0])


def on_device(
    positions, feats, species, pad_count, k_lattice, filter_width, w_charge, species_embed, w_out, grad_out
):
    vmem = pl.BlockSpec(memory_space=pltpu.VMEM)
    dma = pltpu.SemaphoreType.DMA
    regular = pltpu.SemaphoreType.REGULAR
    operands = [
        pltpu.with_memory_space_constraint(array, pltpu.HBM)
        for array in (
            positions, feats, species.reshape(1, -1), pad_count, k_lattice, filter_width.reshape(1, -1),
            w_charge, species_embed.T, w_out, grad_out,
        )
    ]
    shapes = ((CH, S), (3, S), (CH, S))
    results = pl.pallas_call(
        kernel,
        out_shape=tuple(pltpu.VMEM(shape, f32) for shape in shapes),
        in_specs=[pl.BlockSpec(memory_space=pl.ANY)] * 10,
        out_specs=(vmem, vmem, vmem),
        scratch_shapes=[
            pltpu.VMEM((3, 2 * A), f32),
            pltpu.VMEM((CH, 2 * A), f32),
            pltpu.VMEM((1, 2 * A), jnp.int32),
            pltpu.SMEM((8,), jnp.int32),
            pltpu.VMEM((3, H), jnp.int32),
            pltpu.VMEM((1, CH), f32),
            pltpu.VMEM((CH, CH), f32),
            pltpu.VMEM((16, CH), f32),
            pltpu.VMEM((CH, CH), f32),
            pltpu.VMEM((2, 8, H), f32),
            pltpu.VMEM((K, 8), f32),
            pltpu.VMEM((K, 32), bf16),
            pltpu.VMEM((2, 32, A), bf16),
            pltpu.VMEM((2, 1, A), f32),
            pltpu.VMEM((2 * K, A), bf16),
            pltpu.VMEM((2 * K, A), bf16),
            pltpu.VMEM((2 * H, A), bf16),
            pltpu.VMEM((2 * H, A), bf16),
            pltpu.VMEM((K, A), f32),
            pltpu.VMEM((K, A), f32),
            pltpu.VMEM((128, A), bf16),
            pltpu.VMEM((128, A), bf16),
            pltpu.VMEM((8, CH, S), f32),
            pltpu.VMEM((128, A), bf16),
            pltpu.VMEM((H, 128), f32),
            pltpu.VMEM((K, 128), f32),
            pltpu.VMEM((H, 128), f32),
            pltpu.VMEM((K, 128), f32),
            pltpu.VMEM((H, 128), f32),
            pltpu.VMEM((K, 128), f32),
            pltpu.VMEM((16, 16, 128), f32),
            pltpu.VMEM((32, 16, 128), f32),
            pltpu.VMEM((16, 128), f32),
            pltpu.VMEM((2, 4, 8, 16, 128), f32),
            pltpu.VMEM((2, 8, CH, S), f32),
            pltpu.VMEM((2, 8, CH, S), f32),
            pltpu.VMEM((8, 8, S), f32),
            pltpu.VMEM((8, 8, S), f32),
            dma((10,)), dma((2,)), dma((2,)), dma((2,)),
            dma((2,)), dma((3,)), dma((2,)), dma((2, 2)), dma((2,)),
            regular((8,)), regular, regular, regular,
        ],
        name="ewald",
        compiler_params=pltpu.CompilerParams(
            collective_id=0, has_side_effects=True, vmem_limit_bytes=32 * 1024 * 1024
        ),
    )(*operands)
    return pl.pallas_call(
        put_away,
        out_shape=tuple(jax.ShapeDtypeStruct(shape, f32) for shape in shapes),
        in_specs=[vmem] * 3,
        out_specs=(pl.BlockSpec(memory_space=pl.ANY),) * 3,
        scratch_shapes=[dma((3,))],
        name="put_away",
    )(*results)


def put_away(message, force, gfeat, message_out, force_out, gfeat_out, sem):
    copies = [
        pltpu.make_async_copy(src, dst, sem.at[n])
        for n, (src, dst) in enumerate(((message, message_out), (force, force_out), (gfeat, gfeat_out)))
    ]
    for copy in copies:
        copy.start()
    for copy in copies:
        copy.wait()


def solution(mesh):
    placed = (
        P(None, "atoms"),
        P(None, "atoms"),
        P("atoms"),
        P("atoms"),
        P(None, "kvec"),
        P(),
        P(),
        P(),
        P(),
        P(None, ("atoms", "kvec")),
    )
    return jax.shard_map(
        on_device,
        mesh=mesh,
        in_specs=placed,
        out_specs=(P(None, ("atoms", "kvec")),) * 3,
        check_vma=False,
    )
```

```python
import functools
import math

import jax
import jax.numpy as jnp
import numpy as np
from jax import lax
from jax.experimental import pallas as pl
from jax.experimental.pallas import tpu as pltpu
from jax.sharding import PartitionSpec as P

MESH = pl.DeviceIdType.MESH
exact = lax.Precision.HIGHEST
two_pi = 2.0 * math.pi
f32 = jnp.float32
bf16 = jnp.bfloat16

A = 1024
K = 512
H = 256
CH = 64
S = 128


def fit_poly(fn, count, points=2000):
    nodes = 0.25 * (np.cos(np.pi * (np.arange(points) + 0.5) / points) + 1.0) * 0.5
    table = np.vander(nodes / 0.25, count, increasing=True)
    coef = np.linalg.lstsq(table, fn(np.sqrt(nodes)), rcond=None)[0]
    return [float(c) / 0.25**n for n, c in enumerate(coef)]


sin_coef = fit_poly(lambda u: 2.0 * np.sin(np.pi * u) / u, 5)
cos_coef = fit_poly(lambda u: np.cos(np.pi * u), 5)


def horner(coef, sq):
    total = coef[-1]
    for c in coef[-2::-1]:
        total = total * sq + c
    return total


def sin_cos_turns(t):
    u = t - jnp.round(t)
    sq = u * u
    twice_sin = u * horner(sin_coef, sq)
    cos_half = horner(cos_coef, sq)
    return 1.0 - 0.5 * (twice_sin * twice_sin), twice_sin * cos_half


def split(value):
    high = value.astype(bf16)
    return high, (value - high.astype(f32)).astype(bf16)


def dot(a, b, dims=((1,), (0,)), precision=None):
    return lax.dot_general(a, b, (dims, ((), ())), precision=precision, preferred_element_type=f32)


def ring(d, n):
    return min(d, n - d)


y_steps = sorted(range(1, 8), key=lambda d: -ring(d, 8))
plane_steps = sorted(
    [(dx, dz) for dx in range(4) for dz in range(8) if dx or dz],
    key=lambda d: -(ring(d[0], 4) + ring(d[1], 8)),
)
plane_far = [int(ring(dz, 8) > 2) for _, dz in plane_steps]
y_order = (0, 1, 7, 2, 6, 3, 5, 4)


def kernel(
    pos_hbm, feats_hbm, species_hbm, pad_hbm, k_hbm, width_hbm, wq_hbm, embed_hbm, wo_hbm, grad_hbm,
    message_ref, force_ref, gfeat_ref,
    pos_ref, feats, species_ref, pad_ref, k_ref, width_ref, wq_ref, embed_ref, wo_ref,
    kall, kcol, kmat, xmat, mask, t_hi, t_lo, e_hi, e_lo, cos_f, sin_f, charge, far_charge, cots, adjoint,
    part_h, part_e, in_h, in_e, sum_h, sum_e, ring_h, ring_e, owned, table, out_y, in_y, out_f, in_f,
    load_sem, k_sem, cot_send, cot_recv, core_sem, plane_sem, table_sem, share_sem, y_sem, f_sem,
    y_ready, plane_ready, k_ready, core_ready,
):
    atoms_at = lax.axis_index("atoms")
    kvec_at = lax.axis_index("kvec")
    core, z, x_hi = atoms_at % 2, (atoms_at // 2) % 8, atoms_at // 16
    x_lo, y = kvec_at // 8, kvec_at % 8
    x = x_hi * 2 + x_lo
    me = z * 4 + x
    group_me = x_hi * 8 + z
    x_at = x_lo * 2 + x_hi
    place = x_at * 8 + z

    def on_y(other):
        return (atoms_at, x_lo * 8 + other)

    def on_plane(px, pz):
        return ((px // 2) * 16 + pz * 2 + core, (px % 2) * 8 + y)

    def on_start(p):
        return on_plane(p % 4, p // 4)

    y_peers = [((y + d) % 8, on_y((y + d) % 8)) for d in y_steps]
    plane_peers = []
    group_peers = []
    for dx, dz in plane_steps:
        px, pz = (x + dx) % 4, (z + dz) % 8
        plane_peers.append((((px % 2) * 2 + px // 2) * 8 + pz, on_plane(px, pz)))
        if dx % 2 == 0:
            group_peers.append(((px // 2) * 8 + pz, on_plane(px, pz)))
    sibling = (atoms_at + 1 - 2 * core, kvec_at)
    partner = (atoms_at, (1 - x_lo) * 8 + y)

    def remote(src, dst, send, recv, device):
        return pltpu.make_async_remote_copy(
            src_ref=src, dst_ref=dst, send_sem=send, recv_sem=recv, device_id=device, device_id_type=MESH
        )

    def signal(sem, device):
        pl.semaphore_signal(sem, inc=1, device_id=device, device_id_type=MESH)

    def wait_bytes(ref, sem):
        pltpu.make_async_copy(ref, ref, sem).wait()

    barrier = pltpu.get_barrier_semaphore()
    late = y // 5
    y_rank = (1 - late) * (2 * y - 1) + late * (16 - 2 * y)
    y_before = y_rank + (8 - y) // 8
    for i, other in enumerate(y_order):
        if i:

            @pl.when(i > y_rank)
            def _(other=other):
                signal(barrier, on_y(other))

    lax.fori_loop(me + 1, 32, lambda p, _: (signal(barrier, on_start(p)), 0)[1], 0)

    @pl.when(core == 1)
    def _():
        signal(barrier, sibling)

    loads = {}
    for n, (name, src, dst) in enumerate([
        ("k", k_hbm, k_ref),
        ("pos", pos_hbm, pos_ref),
        ("pad", pad_hbm, pad_ref),
        ("feats", feats_hbm, feats),
        ("species", species_hbm, species_ref),
        ("wq", wq_hbm, wq_ref),
        ("embed", embed_hbm, embed_ref),
        ("wo", wo_hbm, wo_ref),
        ("width", width_hbm, width_ref),
        ("grad", grad_hbm, cots.at[y]),
    ]):
        loads[name] = pltpu.make_async_copy(src, dst, load_sem.at[n])
        loads[name].start()

    before = y_before + me + 1 - core

    @pl.when(before > 0)
    def _():
        pl.semaphore_wait(barrier, before)

    for i, other in enumerate(y_order[:-1]):

        @pl.when(i < y_rank)
        def _(other=other):
            signal(y_ready.at[y], on_y(other))

    @pl.when(x_lo == 1)
    def _():
        signal(k_ready, partner)

    def cot_copy(src, slot, other):
        return remote(src, cots.at[slot], cot_send, cot_recv.at[slot], on_y(other))

    def near(other):
        return (other - y + 10) % 8 <= 4

    for i, other in enumerate(y_order[:-1]):

        @pl.when((i < y_rank) & near(other))
        def _(other=other):
            cot_copy(grad_hbm, y, other).start()

    @pl.when(core == 0)
    def _():
        signal(core_ready, sibling)

    loads["k"].wait()
    kall[x_lo] = jnp.concatenate([k_ref[...].astype(f32), jnp.zeros((5, H), f32)], axis=0)
    k_copy = remote(kall.at[x_lo], kall.at[x_lo], k_sem.at[0], k_sem.at[1], partner)

    @pl.when(x_lo == 1)
    def _():
        k_copy.start()

    lax.fori_loop(0, me, lambda p, _: (signal(plane_ready, on_start(p)), 0)[1], 0)

    halves = [pl.ds(pl.multiple_of(h * A, A), A) for h in (x_lo, 1 - x_lo)]
    loads["pos"].wait()
    loads["pad"].wait()
    lanes = lax.broadcasted_iota(jnp.int32, (1, 256), 1)
    for n, h in enumerate((x_lo, 1 - x_lo)):
        pos = jnp.concatenate([pos_ref[:, halves[n]], jnp.zeros((5, A), f32)], axis=0)
        pos_hi = pos.astype(bf16).astype(f32)
        pos_mid = (pos - pos_hi).astype(bf16).astype(f32)
        pos_low = (pos - pos_hi) - pos_mid
        xmat[n] = jnp.concatenate([pos_hi, pos_mid, pos_low, jnp.zeros((8, A), f32)], axis=0).astype(bf16)
        for block in range(4):
            mask[n, :, block * 256 : (block + 1) * 256] = (lanes < pad_ref[h * 4 + block]).astype(f32)

    def set_k(q):
        kt = kall[q].T
        kcol[pl.ds(pl.multiple_of(q * H, H), H), :] = kt
        kmat[pl.ds(pl.multiple_of(q * H, H), H), :] = jnp.concatenate([kt] * 4, axis=1).astype(bf16)

    def trig(q, n, high_ref, low_ref, cos_base, sin_base, keep):
        def step(i, _):
            rows = pl.ds(pl.multiple_of(q * H + i * 32, 32), 32)
            cos_rows = pl.ds(pl.multiple_of(cos_base + i * 32, 32), 32)
            sin_rows = pl.ds(pl.multiple_of(sin_base + i * 32, 32), 32)
            left = kmat[rows, :]
            for at in range(4):
                cols = slice(at * 256, (at + 1) * 256)
                cos, sin = sin_cos_turns(dot(left, xmat[n, :, cols]))
                if keep:
                    cos_f[rows, cols] = cos
                    sin_f[rows, cols] = sin
                high_ref[cos_rows, cols], low_ref[cos_rows, cols] = split(cos)
                high_ref[sin_rows, cols], low_ref[sin_rows, cols] = split(sin)
            return 0

        lax.fori_loop(0, H // 32, step, 0)

    low_lanes = lax.broadcasted_iota(jnp.int32, (1, 128), 1) < CH

    def factors(out_ref, base, terms):
        for i in range(2):
            found = []
            for sine in (0, 1):
                one = jnp.zeros((128, 128), f32)
                for high_ref, low_ref, cos_base, sin_base, quant in terms:
                    rows = pl.ds(pl.multiple_of((sin_base if sine else cos_base) + i * 128, 128), 128)
                    one = one + dot(high_ref[rows, :], quant[...], ((1,), (1,)))
                    one = one + dot(low_ref[rows, :], quant[...], ((1,), (1,)))
                found.append(one + pltpu.roll(one, CH, 1))
            out_ref[pl.ds(pl.multiple_of(base + i * 128, 128), 128), :] = jnp.where(low_lanes, found[0], found[1])

    set_k(x_lo)
    trig(x_lo, 0, t_hi, t_lo, x_lo * H, K + x_lo * H, True)

    @pl.when(x_lo == 0)
    def _():
        pl.semaphore_wait(k_ready, 1)
        k_copy.start()

    for i, other in enumerate(y_order):
        if i:

            @pl.when((i > y_rank) & near(other))
            def _(other=other):
                pl.semaphore_wait(y_ready.at[other], 1)
                cot_copy(grad_hbm, y, other).start()

    for name in ("feats", "species", "wq", "embed"):
        loads[name].wait()
    for n, quant in enumerate((charge, far_charge)):
        one_hot = (lax.broadcasted_iota(jnp.int32, (16, A), 0) == species_ref[:, halves[n]]).astype(f32)
        quant[0:CH, :], quant[CH:128, :] = split(
            mask[n]
            * (
                dot(wq_ref[...], feats[:, halves[n]], ((0,), (0,)), exact)
                + dot(embed_ref[...], one_hot, ((0,), (0,)), exact)
            )
        )

    def rank_of(other):
        late = other // 5
        return (1 - late) * (2 * other - 1) + late * (16 - 2 * other)

    def cot_wait(slot):
        wait_bytes(cots.at[slot], cot_recv.at[slot])

    def pass_on(back, targets):
        slot = (y + back) % 8
        cot_wait(slot)
        for step in targets:
            cot_copy(cots.at[slot], slot, (y + step) % 8).start()

    routes = ((6, (2, 1)), (2, (7,)))
    for back, targets in routes:

        @pl.when(rank_of((y + back) % 8) < y_rank)
        def _(back=back, targets=targets):
            pass_on(back, targets)

    trig(x_lo, 1, e_hi, e_lo, 0, H, False)

    for back, targets in routes:

        @pl.when(rank_of((y + back) % 8) > y_rank)
        def _(back=back, targets=targets):
            pass_on(back, targets)

    factors(
        part_h, 0, [(t_hi, t_lo, x_lo * H, K + x_lo * H, charge), (e_hi, e_lo, 0, H, far_charge)]
    )

    h_pair = remote(part_h, in_h, core_sem.at[0], core_sem.at[1], sibling)

    @pl.when(core == 1)
    def _():
        pl.semaphore_wait(core_ready, 1)
        h_pair.start()

    remote(kall.at[1 - x_lo], kall.at[1 - x_lo], k_sem.at[0], k_sem.at[1], partner).wait_recv()
    set_k(1 - x_lo)
    trig(1 - x_lo, 0, t_hi, t_lo, (1 - x_lo) * H, K + (1 - x_lo) * H, True)

    def gain_of(first):
        wave = two_pi * kcol[pl.ds(pl.multiple_of(first, 16), 16), :]
        square = jnp.sum(wave * wave, axis=1, keepdims=True)
        width = width_ref[...]
        width = jnp.concatenate([width, width], axis=1)
        return jnp.exp(-square * width) * 40.0 / (square + 40.0) / 256.0

    def scatter(total, peers, ring_ref, mine):
        for p, device in peers:
            remote(
                total.at[pl.ds(pl.multiple_of(p * 16, 16), 16), :], ring_ref.at[mine],
                plane_sem.at[0], plane_sem.at[1], device,
            ).start()
        ring_ref[mine] = total[pl.ds(pl.multiple_of(mine * 16, 16), 16), :]

    def gather(which, ring_ref, count):
        wait_bytes(ring_ref.at[pl.ds(0, count - 1)], plane_sem.at[1])
        total = ring_ref[0]
        for p in range(1, count):
            total = total + ring_ref[p]
        owned[...] = gain_of(place * 16) * total
        for (_, device), far in zip(plane_peers, plane_far):
            remote(owned, table.at[which, x_at, z], table_sem.at[0], table_sem.at[1 + far], device).start()
        table[which, x_at, z] = owned[...]

    def share(which):
        for far, steps in enumerate(((0, 1, 7, 2, 6), (3, 5, 4))):
            wait_bytes(ring_e.at[pl.ds(0, 4 * len(steps) - (1 - far))], table_sem.at[1 + far])
            for step in steps:
                rows = table.at[which, :, (z + step) % 8]
                remote(rows, rows, share_sem.at[0], share_sem.at[1], sibling).start()

    @pl.when(me < 31)
    def _():
        pl.semaphore_wait(plane_ready, 31 - me)

    for i, other in enumerate(y_order):
        if i:

            @pl.when((i > y_rank) & jnp.logical_not(near(other)))
            def _(other=other):
                pl.semaphore_wait(y_ready.at[other], 1)

    for name in ("wo", "width", "grad"):
        loads[name].wait()
    for step in (1, 7, 3, 5, 4):
        cot_wait((y + step) % 8)
    for s in range(8):
        cols = slice(s * S, (s + 1) * S)
        adjoint[0:CH, cols], adjoint[CH:128, cols] = split(
            mask[0, :, cols] * dot(wo_ref[...], cots[s], precision=exact)
        )

    def e_pair(q):
        rows = pl.ds(q * H, H)
        return remote(part_e.at[rows, :], in_e.at[rows, :], core_sem.at[0], core_sem.at[1], sibling)

    for q in range(2):
        factors(part_e, q * H, [(t_hi, t_lo, q * H, K + q * H, adjoint)])

        @pl.when(core == 0)
        def _(q=q):
            e_pair(q).start()

    @pl.when(core == 0)
    def _():
        h_pair.wait_recv()
        sum_h[...] = part_h[...] + in_h[...]
        scatter(sum_h, group_peers, ring_h, group_me)

    @pl.when(core == 1)
    def _():
        wait_bytes(in_e, core_sem.at[1])
        sum_e[...] = part_e[...] + in_e[...]
        scatter(sum_e, plane_peers, ring_e, place)

    @pl.when(core == 0)
    def _():
        gather(0, ring_h, 16)

    @pl.when(core == 1)
    def _():
        gather(1, ring_e, 32)

    def y_copy(which, other):
        return remote(
            out_y.at[which, other], in_y.at[which, y], y_sem.at[0, which], y_sem.at[1, which], on_y(other)
        )

    def fields(which):
        high, low = split(table[which].reshape(K, 128).T)
        left = jnp.concatenate(
            [
                jnp.concatenate([high[0:CH], high[CH:128]], axis=1),
                jnp.concatenate([low[0:CH], low[CH:128]], axis=1),
            ],
            axis=0,
        )
        for turn in (2, 1, 3, 0):
            at = (y // 2 + turn) % 4
            cols = pl.ds(pl.multiple_of(at * 256, 256), 256)
            both = dot(left, t_hi[:, cols]) + dot(left, t_lo[:, cols])
            field = both[0:CH] + both[CH:128]
            for n in range(2):
                other = 2 * at + n
                out_y[which, other] = field[:, n * S : (n + 1) * S]
                if turn:
                    y_copy(which, other).start()
                else:

                    @pl.when(other != y)
                    def _(other=other):
                        y_copy(which, other).start()

        in_y[which, y] = out_y[which, y]

    def forces(which, quant, add):
        high, low = split(table[which].reshape(K, 128))
        high, low = high.astype(f32), low.astype(f32)
        sin_side = jnp.where(low_lanes, pltpu.roll(high, CH, 1), low).astype(bf16)
        cos_side = jnp.where(low_lanes, high, pltpu.roll(low, CH, 1)).astype(bf16)
        sin_side = jnp.concatenate([sin_side, sin_side], axis=1)
        cos_side = jnp.concatenate([cos_side, cos_side], axis=1)
        columns = [kcol[:, n : n + 1] for n in range(3)]
        for at in range(4):
            cols = slice(at * 256, (at + 1) * 256)
            high_q, low_q = quant[0:CH, cols], quant[CH:128, cols]
            right = jnp.concatenate([high_q, high_q, low_q, low_q], axis=0)
            turn = cos_f[:, cols] * dot(sin_side, right) - sin_f[:, cols] * dot(cos_side, right)
            rows = [jnp.sum(column * turn, axis=0, keepdims=True) for column in columns]
            rows = jnp.concatenate(rows + [jnp.zeros((5, 256), f32)], axis=0)
            for half in range(2):
                slot = 2 * at + half
                here = rows[:, half * S : (half + 1) * S]
                out_f[slot] = out_f[slot] + here if add else here

    @pl.when(core == 0)
    def _():
        share(0)

    @pl.when(core == 1)
    def _():
        wait_bytes(table.at[0], share_sem.at[1])

    fields(0)
    forces(0, adjoint, False)

    @pl.when(core == 1)
    def _():
        share(1)

    @pl.when(core == 0)
    def _():
        wait_bytes(table.at[1], share_sem.at[1])

    fields(1)
    forces(1, charge, True)
    for other, device in y_peers:
        remote(out_f.at[other], in_f.at[y], f_sem.at[0], f_sem.at[1], device).start()
    in_f[y] = out_f[y]

    mine = mask[0, :, pl.ds(pl.multiple_of(y * S, S), S)]

    def collect(which):
        wait_bytes(in_y.at[which, pl.ds(0, 7)], y_sem.at[1, which])
        total = in_y[which, 0]
        for s in range(1, 8):
            total = total + in_y[which, s]
        return mine * total

    message_ref[...] = dot(wo_ref[...], collect(0), ((0,), (0,)), exact)
    wait_bytes(in_f.at[pl.ds(0, 7)], f_sem.at[1])
    total = in_f[0]
    for s in range(1, 8):
        total = total + in_f[s]
    force_ref[...] = (two_pi * total)[0:3, :]
    gfeat_ref[...] = dot(wq_ref[...], collect(1), precision=exact)

    k_copy.wait_send()
    wait_bytes(cots.at[pl.ds(0, 7)], cot_send)

    @pl.when(core == 0)
    def _():
        wait_bytes(in_e, core_sem.at[0])
        wait_bytes(ring_h.at[pl.ds(0, 15)], plane_sem.at[0])
        wait_bytes(table.at[0], share_sem.at[0])

    @pl.when(core == 1)
    def _():
        h_pair.wait_send()
        wait_bytes(ring_e.at[pl.ds(0, 31)], plane_sem.at[0])
        wait_bytes(table.at[1], share_sem.at[0])

    wait_bytes(ring_e.at[pl.ds(0, 31)], table_sem.at[0])
    for which in range(2):
        wait_bytes(in_y.at[which, pl.ds(0, 7)], y_sem.at[0, which])
    wait_bytes(in_f.at[pl.ds(0, 7)], f_sem.at[0])


def on_device(
    positions, feats, species, pad_count, k_lattice, filter_width, w_charge, species_embed, w_out, grad_out
):
    vmem = pl.BlockSpec(memory_space=pltpu.VMEM)
    dma = pltpu.SemaphoreType.DMA
    regular = pltpu.SemaphoreType.REGULAR
    operands = [
        pltpu.with_memory_space_constraint(array, pltpu.HBM)
        for array in (
            positions, feats, species.reshape(1, -1), pad_count, k_lattice, filter_width.reshape(1, -1),
            w_charge, species_embed.T, w_out, grad_out,
        )
    ]
    shapes = ((CH, S), (3, S), (CH, S))
    results = pl.pallas_call(
        kernel,
        out_shape=tuple(pltpu.VMEM(shape, f32) for shape in shapes),
        in_specs=[pl.BlockSpec(memory_space=pl.ANY)] * 10,
        out_specs=(vmem, vmem, vmem),
        scratch_shapes=[
            pltpu.VMEM((3, 2 * A), f32),
            pltpu.VMEM((CH, 2 * A), f32),
            pltpu.VMEM((1, 2 * A), jnp.int32),
            pltpu.SMEM((8,), jnp.int32),
            pltpu.VMEM((3, H), jnp.int32),
            pltpu.VMEM((1, CH), f32),
            pltpu.VMEM((CH, CH), f32),
            pltpu.VMEM((16, CH), f32),
            pltpu.VMEM((CH, CH), f32),
            pltpu.VMEM((2, 8, H), f32),
            pltpu.VMEM((K, 8), f32),
            pltpu.VMEM((K, 32), bf16),
            pltpu.VMEM((2, 32, A), bf16),
            pltpu.VMEM((2, 1, A), f32),
            pltpu.VMEM((2 * K, A), bf16),
            pltpu.VMEM((2 * K, A), bf16),
            pltpu.VMEM((2 * H, A), bf16),
            pltpu.VMEM((2 * H, A), bf16),
            pltpu.VMEM((K, A), f32),
            pltpu.VMEM((K, A), f32),
            pltpu.VMEM((128, A), bf16),
            pltpu.VMEM((128, A), bf16),
            pltpu.VMEM((8, CH, S), f32),
            pltpu.VMEM((128, A), bf16),
            pltpu.VMEM((H, 128), f32),
            pltpu.VMEM((K, 128), f32),
            pltpu.VMEM((H, 128), f32),
            pltpu.VMEM((K, 128), f32),
            pltpu.VMEM((H, 128), f32),
            pltpu.VMEM((K, 128), f32),
            pltpu.VMEM((16, 16, 128), f32),
            pltpu.VMEM((32, 16, 128), f32),
            pltpu.VMEM((16, 128), f32),
            pltpu.VMEM((2, 4, 8, 16, 128), f32),
            pltpu.VMEM((2, 8, CH, S), f32),
            pltpu.VMEM((2, 8, CH, S), f32),
            pltpu.VMEM((8, 8, S), f32),
            pltpu.VMEM((8, 8, S), f32),
            dma((10,)), dma((2,)), dma, dma((8,)), dma((2,)),
            dma((2,)), dma((3,)), dma((2,)), dma((2, 2)), dma((2,)),
            regular((8,)), regular, regular, regular,
        ],
        name="ewald",
        compiler_params=pltpu.CompilerParams(
            collective_id=0, has_side_effects=True, vmem_limit_bytes=32 * 1024 * 1024
        ),
    )(*operands)
    return pl.pallas_call(
        put_away,
        out_shape=tuple(jax.ShapeDtypeStruct(shape, f32) for shape in shapes),
        in_specs=[vmem] * 3,
        out_specs=(pl.BlockSpec(memory_space=pl.ANY),) * 3,
        scratch_shapes=[dma((3,))],
        name="put_away",
        compiler_params=pltpu.CompilerParams(vmem_limit_bytes=1024 * 1024),
    )(*[pltpu.with_memory_space_constraint(array, pltpu.VMEM) for array in results])


def put_away(message, force, gfeat, message_out, force_out, gfeat_out, sem):
    copies = [
        pltpu.make_async_copy(src, dst, sem.at[n])
        for n, (src, dst) in enumerate(((message, message_out), (force, force_out), (gfeat, gfeat_out)))
    ]
    for copy in copies:
        copy.start()
    for copy in copies:
        copy.wait()


def solution(mesh):
    placed = (
        P(None, "atoms"),
        P(None, "atoms"),
        P("atoms"),
        P("atoms"),
        P(None, "kvec"),
        P(),
        P(),
        P(),
        P(),
        P(None, ("atoms", "kvec")),
    )
    return jax.shard_map(
        on_device,
        mesh=mesh,
        in_specs=placed,
        out_specs=(P(None, ("atoms", "kvec")),) * 3,
        check_vma=False,
    )
```

```python
import functools
import math

import jax
import jax.numpy as jnp
import numpy as np
from jax import lax
from jax.experimental import pallas as pl
from jax.experimental.pallas import tpu as pltpu
from jax.sharding import PartitionSpec as P

MESH = pl.DeviceIdType.MESH
exact = lax.Precision.HIGHEST
two_pi = 2.0 * math.pi
f32 = jnp.float32
bf16 = jnp.bfloat16

A = 1024
K = 512
H = 256
CH = 64
S = 128


def fit_poly(fn, count, points=2000):
    nodes = 0.25 * (np.cos(np.pi * (np.arange(points) + 0.5) / points) + 1.0) * 0.5
    table = np.vander(nodes / 0.25, count, increasing=True)
    coef = np.linalg.lstsq(table, fn(np.sqrt(nodes)), rcond=None)[0]
    return [float(c) / 0.25**n for n, c in enumerate(coef)]


sin_coef = fit_poly(lambda u: 2.0 * np.sin(np.pi * u) / u, 5)
cos_coef = fit_poly(lambda u: np.cos(np.pi * u), 5)


def horner(coef, sq):
    total = coef[-1]
    for c in coef[-2::-1]:
        total = total * sq + c
    return total


def sin_cos_turns(t):
    u = t - jnp.round(t)
    sq = u * u
    twice_sin = u * horner(sin_coef, sq)
    cos_half = horner(cos_coef, sq)
    return 1.0 - 0.5 * (twice_sin * twice_sin), twice_sin * cos_half


def split(value):
    high = value.astype(bf16)
    return high, (value - high.astype(f32)).astype(bf16)


def dot(a, b, dims=((1,), (0,)), precision=None):
    return lax.dot_general(a, b, (dims, ((), ())), precision=precision, preferred_element_type=f32)


def ring(d, n):
    return min(d, n - d)


y_steps = sorted(range(1, 8), key=lambda d: -ring(d, 8))
plane_steps = sorted(
    [(dx, dz) for dx in range(4) for dz in range(8) if dx or dz],
    key=lambda d: -(ring(d[0], 4) + ring(d[1], 8)),
)
plane_far = [int(ring(dz, 8) > 2) for _, dz in plane_steps]
y_order = (0, 1, 7, 2, 6, 3, 5, 4)


def kernel(
    pos_hbm, feats_hbm, species_hbm, pad_hbm, k_hbm, width_hbm, wq_hbm, embed_hbm, wo_hbm, grad_hbm,
    message_ref, force_ref, gfeat_ref,
    pos_ref, feats, species_ref, pad_ref, k_ref, width_ref, wq_ref, embed_ref, wo_ref,
    kall, kcol, kmat, xmat, mask, t_hi, t_lo, e_hi, e_lo, cos_f, sin_f, quants, far_charge, cots, sums_e,
    part_h, part_e, in_h, in_e, sum_h, sum_e, ring_h, ring_e, owned, table, out_y, in_y, out_f, in_f,
    load_sem, k_sem, cot_send, cot_recv, core_sem, plane_sem, table_sem, share_sem, y_sem, f_sem,
    y_ready, plane_ready, k_ready, core_ready,
):
    atoms_at = lax.axis_index("atoms")
    kvec_at = lax.axis_index("kvec")
    core, z, x_hi = atoms_at % 2, (atoms_at // 2) % 8, atoms_at // 16
    x_lo, y = kvec_at // 8, kvec_at % 8
    x = x_hi * 2 + x_lo
    me = z * 4 + x
    group_me = x_hi * 8 + z
    x_at = x_lo * 2 + x_hi
    place = x_at * 8 + z

    def on_y(other):
        return (atoms_at, x_lo * 8 + other)

    def on_plane(px, pz):
        return ((px // 2) * 16 + pz * 2 + core, (px % 2) * 8 + y)

    def on_start(p):
        return on_plane(p % 4, p // 4)

    y_peers = [((y + d) % 8, on_y((y + d) % 8)) for d in y_steps]
    plane_peers = []
    group_peers = []
    for dx, dz in plane_steps:
        px, pz = (x + dx) % 4, (z + dz) % 8
        plane_peers.append((((px % 2) * 2 + px // 2) * 8 + pz, on_plane(px, pz)))
        if dx % 2 == 0:
            group_peers.append(((px // 2) * 8 + pz, on_plane(px, pz)))
    sibling = (atoms_at + 1 - 2 * core, kvec_at)
    partner = (atoms_at, (1 - x_lo) * 8 + y)

    def remote(src, dst, send, recv, device):
        return pltpu.make_async_remote_copy(
            src_ref=src, dst_ref=dst, send_sem=send, recv_sem=recv, device_id=device, device_id_type=MESH
        )

    def signal(sem, device):
        pl.semaphore_signal(sem, inc=1, device_id=device, device_id_type=MESH)

    def wait_bytes(ref, sem):
        pltpu.make_async_copy(ref, ref, sem).wait()

    barrier = pltpu.get_barrier_semaphore()
    late = y // 5
    y_rank = (1 - late) * (2 * y - 1) + late * (16 - 2 * y)
    y_before = y_rank + (8 - y) // 8
    for i, other in enumerate(y_order):
        if i:

            @pl.when(i > y_rank)
            def _(other=other):
                signal(barrier, on_y(other))

    lax.fori_loop(me + 1, 32, lambda p, _: (signal(barrier, on_start(p)), 0)[1], 0)

    @pl.when(core == 1)
    def _():
        signal(barrier, sibling)

    loads = {}
    for n, (name, src, dst) in enumerate([
        ("k", k_hbm, k_ref),
        ("pos", pos_hbm, pos_ref),
        ("pad", pad_hbm, pad_ref),
        ("feats", feats_hbm, feats),
        ("species", species_hbm, species_ref),
        ("wq", wq_hbm, wq_ref),
        ("embed", embed_hbm, embed_ref),
        ("wo", wo_hbm, wo_ref),
        ("width", width_hbm, width_ref),
        ("grad", grad_hbm, cots.at[y]),
    ]):
        loads[name] = pltpu.make_async_copy(src, dst, load_sem.at[n])
        loads[name].start()

    before = y_before + me + 1 - core

    @pl.when(before > 0)
    def _():
        pl.semaphore_wait(barrier, before)

    for i, other in enumerate(y_order[:-1]):

        @pl.when(i < y_rank)
        def _(other=other):
            signal(y_ready.at[y], on_y(other))

    @pl.when(x_lo == 1)
    def _():
        signal(k_ready, partner)

    def cot_copy(device):
        return remote(grad_hbm, cots.at[y], cot_send, cot_recv.at[y], device)

    for i, other in enumerate(y_order[:-1]):

        @pl.when(i < y_rank)
        def _(other=other):
            cot_copy(on_y(other)).start()

    @pl.when(core == 0)
    def _():
        signal(core_ready, sibling)

    loads["k"].wait()
    kall[x_lo] = jnp.concatenate([k_ref[...].astype(f32), jnp.zeros((5, H), f32)], axis=0)
    k_copy = remote(kall.at[x_lo], kall.at[x_lo], k_sem.at[0], k_sem.at[1], partner)

    @pl.when(x_lo == 1)
    def _():
        k_copy.start()

    lax.fori_loop(0, me, lambda p, _: (signal(plane_ready, on_start(p)), 0)[1], 0)

    halves = [pl.ds(pl.multiple_of(h * A, A), A) for h in (x_lo, 1 - x_lo)]
    loads["pos"].wait()
    loads["pad"].wait()
    lanes = lax.broadcasted_iota(jnp.int32, (1, 256), 1)
    for n, h in enumerate((x_lo, 1 - x_lo)):
        pos = jnp.concatenate([pos_ref[:, halves[n]], jnp.zeros((5, A), f32)], axis=0)
        pos_hi = pos.astype(bf16).astype(f32)
        pos_mid = (pos - pos_hi).astype(bf16).astype(f32)
        pos_low = (pos - pos_hi) - pos_mid
        xmat[n] = jnp.concatenate([pos_hi, pos_mid, pos_low, jnp.zeros((8, A), f32)], axis=0).astype(bf16)
        for block in range(4):
            mask[n, :, block * 256 : (block + 1) * 256] = (lanes < pad_ref[h * 4 + block]).astype(f32)

    def set_k(q):
        kt = kall[q].T
        kcol[pl.ds(pl.multiple_of(q * H, H), H), :] = kt
        kmat[pl.ds(pl.multiple_of(q * H, H), H), :] = jnp.concatenate([kt] * 4, axis=1).astype(bf16)

    def trig(q, n, high_ref, low_ref, cos_base, sin_base, keep):
        def step(i, _):
            rows = pl.ds(pl.multiple_of(q * H + i * 32, 32), 32)
            cos_rows = pl.ds(pl.multiple_of(cos_base + i * 32, 32), 32)
            sin_rows = pl.ds(pl.multiple_of(sin_base + i * 32, 32), 32)
            left = kmat[rows, :]
            for at in range(4):
                cols = slice(at * 256, (at + 1) * 256)
                cos, sin = sin_cos_turns(dot(left, xmat[n, :, cols]))
                if keep:
                    cos_f[rows, cols] = cos
                    sin_f[rows, cols] = sin
                high_ref[cos_rows, cols], low_ref[cos_rows, cols] = split(cos)
                high_ref[sin_rows, cols], low_ref[sin_rows, cols] = split(sin)
            return 0

        lax.fori_loop(0, H // 32, step, 0)

    low_lanes = lax.broadcasted_iota(jnp.int32, (1, 128), 1) < CH

    def factors(out_ref, base, terms):
        for i in range(2):
            found = []
            for sine in (0, 1):
                one = jnp.zeros((128, 128), f32)
                for high_ref, low_ref, cos_base, sin_base, quant in terms:
                    rows = pl.ds(pl.multiple_of((sin_base if sine else cos_base) + i * 128, 128), 128)
                    one = one + dot(high_ref[rows, :], quant[...], ((1,), (1,)))
                    one = one + dot(low_ref[rows, :], quant[...], ((1,), (1,)))
                found.append(one + pltpu.roll(one, CH, 1))
            out_ref[pl.ds(pl.multiple_of(base + i * 128, 128), 128), :] = jnp.where(low_lanes, found[0], found[1])

    set_k(x_lo)
    trig(x_lo, 0, t_hi, t_lo, x_lo * H, K + x_lo * H, True)

    @pl.when(x_lo == 0)
    def _():
        pl.semaphore_wait(k_ready, 1)
        k_copy.start()

    for i, other in enumerate(y_order):
        if i:

            @pl.when(i > y_rank)
            def _(other=other):
                pl.semaphore_wait(y_ready.at[other], 1)
                cot_copy(on_y(other)).start()

    for name in ("feats", "species", "wq", "embed"):
        loads[name].wait()
    for n, quant in enumerate((quants.at[0], far_charge)):
        one_hot = (lax.broadcasted_iota(jnp.int32, (16, A), 0) == species_ref[:, halves[n]]).astype(f32)
        quant[0:CH, :], quant[CH:128, :] = split(
            mask[n]
            * (
                dot(wq_ref[...], feats[:, halves[n]], ((0,), (0,)), exact)
                + dot(embed_ref[...], one_hot, ((0,), (0,)), exact)
            )
        )

    trig(x_lo, 1, e_hi, e_lo, 0, H, False)
    factors(
        part_h, 0, [(t_hi, t_lo, x_lo * H, K + x_lo * H, quants.at[0]), (e_hi, e_lo, 0, H, far_charge)]
    )

    h_pair = remote(part_h, in_h, core_sem.at[0], core_sem.at[1], sibling)

    @pl.when(core == 1)
    def _():
        pl.semaphore_wait(core_ready, 1)
        h_pair.start()

    def gain_of(first):
        wave = two_pi * kcol[pl.ds(pl.multiple_of(first, 16), 16), :]
        square = jnp.sum(wave * wave, axis=1, keepdims=True)
        width = width_ref[...]
        width = jnp.concatenate([width, width], axis=1)
        return jnp.exp(-square * width) * 40.0 / (square + 40.0) / 256.0

    def scatter(total, peers, ring_ref, mine):
        for p, device in peers:
            remote(
                total.at[pl.ds(pl.multiple_of(p * 16, 16), 16), :], ring_ref.at[mine],
                plane_sem.at[0], plane_sem.at[1], device,
            ).start()
        ring_ref[mine] = total[pl.ds(pl.multiple_of(mine * 16, 16), 16), :]

    def gather(which, ring_ref, count):
        wait_bytes(ring_ref.at[pl.ds(0, count - 1)], plane_sem.at[1])
        total = ring_ref[0]
        for p in range(1, count):
            total = total + ring_ref[p]
        owned[...] = gain_of(place * 16) * total
        for (_, device), far in zip(plane_peers, plane_far):
            remote(owned, table.at[which, x_at, z], table_sem.at[0], table_sem.at[1 + far], device).start()
        table[which, x_at, z] = owned[...]

    def share(which):
        for far, steps in enumerate(((0, 1, 7, 2, 6), (3, 5, 4))):
            wait_bytes(ring_e.at[pl.ds(0, 4 * len(steps) - (1 - far))], table_sem.at[1 + far])
            for step in steps:
                rows = table.at[which, :, (z + step) % 8]
                remote(rows, rows, share_sem.at[0], share_sem.at[1], sibling).start()

    @pl.when(me < 31)
    def _():
        pl.semaphore_wait(plane_ready, 31 - me)

    @pl.when(core == 0)
    def _():
        h_pair.wait_recv()
        sum_h[...] = part_h[...] + in_h[...]
        scatter(sum_h, group_peers, ring_h, group_me)

    remote(kall.at[1 - x_lo], kall.at[1 - x_lo], k_sem.at[0], k_sem.at[1], partner).wait_recv()
    set_k(1 - x_lo)
    trig(1 - x_lo, 0, t_hi, t_lo, (1 - x_lo) * H, K + (1 - x_lo) * H, True)

    for name in ("wo", "width", "grad"):
        loads[name].wait()

    def add_pair(turn):
        pair = (y // 2 + turn) % 4
        cols = pl.ds(pl.multiple_of(pair * 256, 256), 256)
        for slot in (2 * pair, 2 * pair + 1):
            if turn:
                wait_bytes(cots.at[slot], cot_recv.at[slot])
            else:

                @pl.when(slot != y)
                def _(slot=slot):
                    wait_bytes(cots.at[slot], cot_recv.at[slot])

        block = jnp.concatenate([cots[2 * pair], cots[2 * pair + 1]], axis=1)
        both = jnp.concatenate(split(mask[0, :, cols] * dot(wo_ref[...], block, precision=exact)), axis=0)
        quants[1, :, cols] = both
        for sine in range(2):
            for i in range(4):
                rows = slice(sine * K + i * 128, sine * K + (i + 1) * 128)
                here = slice(i * 128, (i + 1) * 128)
                one = dot(t_hi[rows, cols], both, ((1,), (1,))) + dot(t_lo[rows, cols], both, ((1,), (1,)))
                sums_e[sine, here, :] = one + sums_e[sine, here, :] if turn else one

    for turn in (0, 1, 3, 2):
        add_pair(turn)

    def e_pair(q):
        rows = pl.ds(q * H, H)
        return remote(part_e.at[rows, :], in_e.at[rows, :], core_sem.at[0], core_sem.at[1], sibling)

    for q in range(2):
        rows = slice(q * H, (q + 1) * H)
        found = [sums_e[sine, rows, :] for sine in range(2)]
        found = [one + pltpu.roll(one, CH, 1) for one in found]
        part_e[rows, :] = jnp.where(low_lanes, found[0], found[1])

        @pl.when(core == 0)
        def _(q=q):
            e_pair(q).start()

    @pl.when(core == 1)
    def _():
        wait_bytes(in_e, core_sem.at[1])
        sum_e[...] = part_e[...] + in_e[...]
        scatter(sum_e, plane_peers, ring_e, place)

    @pl.when(core == 0)
    def _():
        gather(0, ring_h, 16)

    @pl.when(core == 1)
    def _():
        gather(1, ring_e, 32)

    def y_copy(which, other):
        return remote(
            out_y.at[which, other], in_y.at[which, y], y_sem.at[0, which], y_sem.at[1, which], on_y(other)
        )

    def fields(which):
        high, low = split(table[which].reshape(K, 128).T)
        left = jnp.concatenate(
            [
                jnp.concatenate([high[0:CH], high[CH:128]], axis=1),
                jnp.concatenate([low[0:CH], low[CH:128]], axis=1),
            ],
            axis=0,
        )
        for turn in (2, 1, 3, 0):
            at = (y // 2 + turn) % 4
            cols = pl.ds(pl.multiple_of(at * 256, 256), 256)
            both = dot(left, t_hi[:, cols]) + dot(left, t_lo[:, cols])
            field = both[0:CH] + both[CH:128]
            for n in range(2):
                other = 2 * at + n
                out_y[which, other] = field[:, n * S : (n + 1) * S]
                if turn:
                    y_copy(which, other).start()
                else:

                    @pl.when(other != y)
                    def _(other=other):
                        y_copy(which, other).start()

        in_y[which, y] = out_y[which, y]

    def forces(which, add):
        high, low = split(table[which].reshape(K, 128))
        high, low = high.astype(f32), low.astype(f32)
        sin_side = jnp.where(low_lanes, pltpu.roll(high, CH, 1), low).astype(bf16)
        cos_side = jnp.where(low_lanes, high, pltpu.roll(low, CH, 1)).astype(bf16)
        sin_side = jnp.concatenate([sin_side, sin_side], axis=1)
        cos_side = jnp.concatenate([cos_side, cos_side], axis=1)
        columns = [kcol[:, n : n + 1] for n in range(3)]
        for at in range(4):
            cols = slice(at * 256, (at + 1) * 256)
            high_q, low_q = quants[1 - which, 0:CH, cols], quants[1 - which, CH:128, cols]
            right = jnp.concatenate([high_q, high_q, low_q, low_q], axis=0)
            turn = cos_f[:, cols] * dot(sin_side, right) - sin_f[:, cols] * dot(cos_side, right)
            rows = [jnp.sum(column * turn, axis=0, keepdims=True) for column in columns]
            rows = jnp.concatenate(rows + [jnp.zeros((5, 256), f32)], axis=0)
            for half in range(2):
                slot = 2 * at + half
                here = rows[:, half * S : (half + 1) * S]
                out_f[slot] = out_f[slot] + here if add else here

    share(core)
    fields(core)
    forces(core, False)
    wait_bytes(table.at[1 - core], share_sem.at[1])
    fields(1 - core)
    forces(1 - core, True)
    for other, device in y_peers:
        remote(out_f.at[other], in_f.at[y], f_sem.at[0], f_sem.at[1], device).start()
    in_f[y] = out_f[y]

    mine = mask[0, :, pl.ds(pl.multiple_of(y * S, S), S)]

    def collect(which):
        wait_bytes(in_y.at[which, pl.ds(0, 7)], y_sem.at[1, which])
        total = in_y[which, 0]
        for s in range(1, 8):
            total = total + in_y[which, s]
        return mine * total

    message_ref[...] = dot(wo_ref[...], collect(0), ((0,), (0,)), exact)
    wait_bytes(in_f.at[pl.ds(0, 7)], f_sem.at[1])
    total = in_f[0]
    for s in range(1, 8):
        total = total + in_f[s]
    force_ref[...] = (two_pi * total)[0:3, :]
    gfeat_ref[...] = dot(wq_ref[...], collect(1), precision=exact)

    k_copy.wait_send()
    wait_bytes(cots.at[pl.ds(0, 7)], cot_send)

    @pl.when(core == 0)
    def _():
        wait_bytes(in_e, core_sem.at[0])
        wait_bytes(ring_h.at[pl.ds(0, 15)], plane_sem.at[0])

    @pl.when(core == 1)
    def _():
        h_pair.wait_send()
        wait_bytes(ring_e.at[pl.ds(0, 31)], plane_sem.at[0])

    wait_bytes(ring_e.at[pl.ds(0, 31)], table_sem.at[0])
    wait_bytes(table.at[core], share_sem.at[0])
    for which in range(2):
        wait_bytes(in_y.at[which, pl.ds(0, 7)], y_sem.at[0, which])
    wait_bytes(in_f.at[pl.ds(0, 7)], f_sem.at[0])


def on_device(
    positions, feats, species, pad_count, k_lattice, filter_width, w_charge, species_embed, w_out, grad_out
):
    vmem = pl.BlockSpec(memory_space=pltpu.VMEM)
    dma = pltpu.SemaphoreType.DMA
    regular = pltpu.SemaphoreType.REGULAR
    operands = [
        pltpu.with_memory_space_constraint(array, pltpu.HBM)
        for array in (
            positions, feats, species.reshape(1, -1), pad_count, k_lattice, filter_width.reshape(1, -1),
            w_charge, species_embed.T, w_out, grad_out,
        )
    ]
    shapes = ((CH, S), (3, S), (CH, S))
    results = pl.pallas_call(
        kernel,
        out_shape=tuple(pltpu.VMEM(shape, f32) for shape in shapes),
        in_specs=[pl.BlockSpec(memory_space=pl.ANY)] * 10,
        out_specs=(vmem, vmem, vmem),
        scratch_shapes=[
            pltpu.VMEM((3, 2 * A), f32),
            pltpu.VMEM((CH, 2 * A), f32),
            pltpu.VMEM((1, 2 * A), jnp.int32),
            pltpu.SMEM((8,), jnp.int32),
            pltpu.VMEM((3, H), jnp.int32),
            pltpu.VMEM((1, CH), f32),
            pltpu.VMEM((CH, CH), f32),
            pltpu.VMEM((16, CH), f32),
            pltpu.VMEM((CH, CH), f32),
            pltpu.VMEM((2, 8, H), f32),
            pltpu.VMEM((K, 8), f32),
            pltpu.VMEM((K, 32), bf16),
            pltpu.VMEM((2, 32, A), bf16),
            pltpu.VMEM((2, 1, A), f32),
            pltpu.VMEM((2 * K, A), bf16),
            pltpu.VMEM((2 * K, A), bf16),
            pltpu.VMEM((2 * H, A), bf16),
            pltpu.VMEM((2 * H, A), bf16),
            pltpu.VMEM((K, A), f32),
            pltpu.VMEM((K, A), f32),
            pltpu.VMEM((2, 128, A), bf16),
            pltpu.VMEM((128, A), bf16),
            pltpu.VMEM((8, CH, S), f32),
            pltpu.VMEM((2, K, 128), f32),
            pltpu.VMEM((H, 128), f32),
            pltpu.VMEM((K, 128), f32),
            pltpu.VMEM((H, 128), f32),
            pltpu.VMEM((K, 128), f32),
            pltpu.VMEM((H, 128), f32),
            pltpu.VMEM((K, 128), f32),
            pltpu.VMEM((16, 16, 128), f32),
            pltpu.VMEM((32, 16, 128), f32),
            pltpu.VMEM((16, 128), f32),
            pltpu.VMEM((2, 4, 8, 16, 128), f32),
            pltpu.VMEM((2, 8, CH, S), f32),
            pltpu.VMEM((2, 8, CH, S), f32),
            pltpu.VMEM((8, 8, S), f32),
            pltpu.VMEM((8, 8, S), f32),
            dma((10,)), dma((2,)), dma, dma((8,)), dma((2,)),
            dma((2,)), dma((3,)), dma((2,)), dma((2, 2)), dma((2,)),
            regular((8,)), regular, regular, regular,
        ],
        name="ewald",
        compiler_params=pltpu.CompilerParams(
            collective_id=0, has_side_effects=True, vmem_limit_bytes=32 * 1024 * 1024
        ),
    )(*operands)
    return pl.pallas_call(
        put_away,
        out_shape=tuple(jax.ShapeDtypeStruct(shape, f32) for shape in shapes),
        in_specs=[vmem] * 3,
        out_specs=(pl.BlockSpec(memory_space=pl.ANY),) * 3,
        scratch_shapes=[dma((3,))],
        name="put_away",
        compiler_params=pltpu.CompilerParams(vmem_limit_bytes=1024 * 1024),
    )(*[pltpu.with_memory_space_constraint(array, pltpu.VMEM) for array in results])


def put_away(message, force, gfeat, message_out, force_out, gfeat_out, sem):
    copies = [
        pltpu.make_async_copy(src, dst, sem.at[n])
        for n, (src, dst) in enumerate(((message, message_out), (force, force_out), (gfeat, gfeat_out)))
    ]
    for copy in copies:
        copy.start()
    for copy in copies:
        copy.wait()


def solution(mesh):
    placed = (
        P(None, "atoms"),
        P(None, "atoms"),
        P("atoms"),
        P("atoms"),
        P(None, "kvec"),
        P(),
        P(),
        P(),
        P(),
        P(None, ("atoms", "kvec")),
    )
    return jax.shard_map(
        on_device,
        mesh=mesh,
        in_specs=placed,
        out_specs=(P(None, ("atoms", "kvec")),) * 3,
        check_vma=False,
    )
```

```python
import functools
import math

import jax
import jax.numpy as jnp
import numpy as np
from jax import lax
from jax.experimental import pallas as pl
from jax.experimental.pallas import tpu as pltpu
from jax.sharding import PartitionSpec as P

MESH = pl.DeviceIdType.MESH
exact = lax.Precision.HIGHEST
two_pi = 2.0 * math.pi
f32 = jnp.float32
bf16 = jnp.bfloat16

A = 1024
K = 512
H = 256
CH = 64
S = 128


def fit_poly(fn, count, points=2000):
    nodes = 0.25 * (np.cos(np.pi * (np.arange(points) + 0.5) / points) + 1.0) * 0.5
    table = np.vander(nodes / 0.25, count, increasing=True)
    coef = np.linalg.lstsq(table, fn(np.sqrt(nodes)), rcond=None)[0]
    return [float(c) / 0.25**n for n, c in enumerate(coef)]


sin_coef = fit_poly(lambda u: 2.0 * np.sin(np.pi * u) / u, 5)
cos_coef = fit_poly(lambda u: np.cos(np.pi * u), 5)


def horner(coef, sq):
    total = coef[-1]
    for c in coef[-2::-1]:
        total = total * sq + c
    return total


def sin_cos_turns(t):
    u = t - jnp.round(t)
    sq = u * u
    twice_sin = u * horner(sin_coef, sq)
    cos_half = horner(cos_coef, sq)
    return 1.0 - 0.5 * (twice_sin * twice_sin), twice_sin * cos_half


def split(value):
    high = value.astype(bf16)
    return high, (value - high.astype(f32)).astype(bf16)


def dot(a, b, dims=((1,), (0,)), precision=None):
    return lax.dot_general(a, b, (dims, ((), ())), precision=precision, preferred_element_type=f32)


def ring(d, n):
    return min(d, n - d)


y_steps = sorted(range(1, 8), key=lambda d: -ring(d, 8))
plane_steps = sorted(
    [(dx, dz) for dx in range(4) for dz in range(8) if dx or dz],
    key=lambda d: -(ring(d[0], 4) + ring(d[1], 8)),
)
plane_far = [int(ring(dz, 8) > 2) for _, dz in plane_steps]
y_order = (0, 1, 7, 2, 6, 3, 5, 4)


def kernel(
    pos_hbm, feats_hbm, species_hbm, pad_hbm, k_hbm, width_hbm, wq_hbm, embed_hbm, wo_hbm, grad_hbm,
    message_ref, force_ref, gfeat_ref,
    pos_ref, feats, species_ref, pad_ref, k_ref, width_ref, wq_ref, embed_ref, wo_ref,
    kall, kcol, kmat, xmat, mask, t_hi, t_lo, e_hi, e_lo, cos_f, sin_f, quants, far_charge, cots, sums_e,
    part_h, part_e, in_h, in_e, sum_h, sum_e, ring_h, ring_e, owned, table, out_y, in_y, out_f, in_f,
    load_sem, k_sem, cot_send, cot_recv, core_sem, plane_sem, table_sem, share_sem, y_sem, f_sem,
    y_ready, plane_ready, k_ready, core_ready,
):
    atoms_at = lax.axis_index("atoms")
    kvec_at = lax.axis_index("kvec")
    core, z, x_hi = atoms_at % 2, (atoms_at // 2) % 8, atoms_at // 16
    x_lo, y = kvec_at // 8, kvec_at % 8
    x = x_hi * 2 + x_lo
    me = z * 4 + x
    group_me = x_hi * 8 + z
    x_at = x_lo * 2 + x_hi
    place = x_at * 8 + z

    def on_y(other):
        return (atoms_at, x_lo * 8 + other)

    def on_plane(px, pz):
        return ((px // 2) * 16 + pz * 2 + core, (px % 2) * 8 + y)

    def on_start(p):
        return on_plane(p % 4, p // 4)

    y_peers = [((y + d) % 8, on_y((y + d) % 8)) for d in y_steps]
    plane_peers = []
    group_peers = []
    for dx, dz in plane_steps:
        px, pz = (x + dx) % 4, (z + dz) % 8
        plane_peers.append((((px % 2) * 2 + px // 2) * 8 + pz, on_plane(px, pz)))
        if dx % 2 == 0:
            group_peers.append(((px // 2) * 8 + pz, on_plane(px, pz)))
    sibling = (atoms_at + 1 - 2 * core, kvec_at)
    partner = (atoms_at, (1 - x_lo) * 8 + y)

    def remote(src, dst, send, recv, device):
        return pltpu.make_async_remote_copy(
            src_ref=src, dst_ref=dst, send_sem=send, recv_sem=recv, device_id=device, device_id_type=MESH
        )

    def signal(sem, device):
        pl.semaphore_signal(sem, inc=1, device_id=device, device_id_type=MESH)

    def wait_bytes(ref, sem):
        pltpu.make_async_copy(ref, ref, sem).wait()

    barrier = pltpu.get_barrier_semaphore()
    late = y // 5
    y_rank = (1 - late) * (2 * y - 1) + late * (16 - 2 * y)
    y_before = y_rank + (8 - y) // 8
    for i, other in enumerate(y_order):
        if i:

            @pl.when(i > y_rank)
            def _(other=other):
                signal(barrier, on_y(other))

    lax.fori_loop(me + 1, 32, lambda p, _: (signal(barrier, on_start(p)), 0)[1], 0)

    @pl.when(core == 1)
    def _():
        signal(barrier, sibling)

    loads = {}
    for n, (name, src, dst) in enumerate([
        ("k", k_hbm, k_ref),
        ("pos", pos_hbm, pos_ref),
        ("pad", pad_hbm, pad_ref),
        ("feats", feats_hbm, feats),
        ("species", species_hbm, species_ref),
        ("wq", wq_hbm, wq_ref),
        ("embed", embed_hbm, embed_ref),
        ("wo", wo_hbm, wo_ref),
        ("width", width_hbm, width_ref),
        ("grad", grad_hbm, cots.at[y]),
    ]):
        loads[name] = pltpu.make_async_copy(src, dst, load_sem.at[n])
        loads[name].start()

    before = y_before + me + 1 - core

    @pl.when(before > 0)
    def _():
        pl.semaphore_wait(barrier, before)

    for i, other in enumerate(y_order[:-1]):

        @pl.when(i < y_rank)
        def _(other=other):
            signal(y_ready.at[y], on_y(other))

    @pl.when(x_lo == 1)
    def _():
        signal(k_ready, partner)

    def cot_copy(device):
        return remote(grad_hbm, cots.at[y], cot_send, cot_recv.at[y], device)

    for i, other in enumerate(y_order[:-1]):

        @pl.when(i < y_rank)
        def _(other=other):
            cot_copy(on_y(other)).start()

    @pl.when(core == 0)
    def _():
        signal(core_ready, sibling)

    loads["k"].wait()
    kall[x_lo] = jnp.concatenate([k_ref[...].astype(f32), jnp.zeros((5, H), f32)], axis=0)
    k_copy = remote(kall.at[x_lo], kall.at[x_lo], k_sem.at[0], k_sem.at[1], partner)

    @pl.when(x_lo == 1)
    def _():
        k_copy.start()

    lax.fori_loop(0, me, lambda p, _: (signal(plane_ready, on_start(p)), 0)[1], 0)

    halves = [pl.ds(pl.multiple_of(h * A, A), A) for h in (x_lo, 1 - x_lo)]
    loads["pos"].wait()
    loads["pad"].wait()
    lanes = lax.broadcasted_iota(jnp.int32, (1, 256), 1)
    for n, h in enumerate((x_lo, 1 - x_lo)):
        pos = jnp.concatenate([pos_ref[:, halves[n]], jnp.zeros((5, A), f32)], axis=0)
        pos_hi = pos.astype(bf16).astype(f32)
        pos_mid = (pos - pos_hi).astype(bf16).astype(f32)
        pos_low = (pos - pos_hi) - pos_mid
        xmat[n] = jnp.concatenate([pos_hi, pos_mid, pos_low, jnp.zeros((8, A), f32)], axis=0).astype(bf16)
        for block in range(4):
            mask[n, :, block * 256 : (block + 1) * 256] = (lanes < pad_ref[h * 4 + block]).astype(f32)

    def set_k(q):
        kt = kall[q].T
        kcol[pl.ds(pl.multiple_of(q * H, H), H), :] = kt
        kmat[pl.ds(pl.multiple_of(q * H, H), H), :] = jnp.concatenate([kt] * 4, axis=1).astype(bf16)

    def trig(q, n, high_ref, low_ref, cos_base, sin_base, keep):
        def step(i, _):
            rows = pl.ds(pl.multiple_of(q * H + i * 128, 128), 128)
            cos_rows = pl.ds(pl.multiple_of(cos_base + i * 128, 128), 128)
            sin_rows = pl.ds(pl.multiple_of(sin_base + i * 128, 128), 128)
            left = kmat[rows, :]
            for at in range(4):
                cols = slice(at * 256, (at + 1) * 256)
                cos, sin = sin_cos_turns(dot(left, xmat[n, :, cols]))
                if keep:
                    cos_f[rows, cols] = cos
                    sin_f[rows, cols] = sin
                high_ref[cos_rows, cols], low_ref[cos_rows, cols] = split(cos)
                high_ref[sin_rows, cols], low_ref[sin_rows, cols] = split(sin)
            return 0

        lax.fori_loop(0, H // 128, step, 0)

    low_lanes = lax.broadcasted_iota(jnp.int32, (1, 128), 1) < CH

    def factors(out_ref, base, terms):
        for i in range(2):
            found = []
            for sine in (0, 1):
                one = jnp.zeros((128, 128), f32)
                for high_ref, low_ref, cos_base, sin_base, quant in terms:
                    rows = pl.ds(pl.multiple_of((sin_base if sine else cos_base) + i * 128, 128), 128)
                    one = one + dot(high_ref[rows, :], quant[...], ((1,), (1,)))
                    one = one + dot(low_ref[rows, :], quant[...], ((1,), (1,)))
                found.append(one + pltpu.roll(one, CH, 1))
            out_ref[pl.ds(pl.multiple_of(base + i * 128, 128), 128), :] = jnp.where(low_lanes, found[0], found[1])

    set_k(x_lo)
    trig(x_lo, 0, t_hi, t_lo, x_lo * H, K + x_lo * H, True)

    @pl.when(x_lo == 0)
    def _():
        pl.semaphore_wait(k_ready, 1)
        k_copy.start()

    for i, other in enumerate(y_order):
        if i:

            @pl.when(i > y_rank)
            def _(other=other):
                pl.semaphore_wait(y_ready.at[other], 1)
                cot_copy(on_y(other)).start()

    for name in ("feats", "species", "wq", "embed"):
        loads[name].wait()
    for n, quant in enumerate((quants.at[0], far_charge)):
        one_hot = (lax.broadcasted_iota(jnp.int32, (16, A), 0) == species_ref[:, halves[n]]).astype(f32)
        quant[0:CH, :], quant[CH:128, :] = split(
            mask[n]
            * (
                dot(wq_ref[...], feats[:, halves[n]], ((0,), (0,)), exact)
                + dot(embed_ref[...], one_hot, ((0,), (0,)), exact)
            )
        )

    trig(x_lo, 1, e_hi, e_lo, 0, H, False)
    factors(
        part_h, 0, [(t_hi, t_lo, x_lo * H, K + x_lo * H, quants.at[0]), (e_hi, e_lo, 0, H, far_charge)]
    )

    h_pair = remote(part_h, in_h, core_sem.at[0], core_sem.at[1], sibling)

    @pl.when(core == 1)
    def _():
        pl.semaphore_wait(core_ready, 1)
        h_pair.start()

    def gain_of(first):
        wave = two_pi * kcol[pl.ds(pl.multiple_of(first, 16), 16), :]
        square = jnp.sum(wave * wave, axis=1, keepdims=True)
        width = width_ref[...]
        width = jnp.concatenate([width, width], axis=1)
        return jnp.exp(-square * width) * 40.0 / (square + 40.0) / 256.0

    def scatter(total, peers, ring_ref, mine):
        for p, device in peers:
            remote(
                total.at[pl.ds(pl.multiple_of(p * 16, 16), 16), :], ring_ref.at[mine],
                plane_sem.at[0], plane_sem.at[1], device,
            ).start()
        ring_ref[mine] = total[pl.ds(pl.multiple_of(mine * 16, 16), 16), :]

    def gather(which, ring_ref, count):
        wait_bytes(ring_ref.at[pl.ds(0, count - 1)], plane_sem.at[1])
        total = ring_ref[0]
        for p in range(1, count):
            total = total + ring_ref[p]
        owned[...] = gain_of(place * 16) * total
        for (_, device), far in zip(plane_peers, plane_far):
            remote(owned, table.at[which, x_at, z], table_sem.at[0], table_sem.at[1 + far], device).start()
        table[which, x_at, z] = owned[...]

    def share(which):
        for far, steps in enumerate(((0, 1, 7, 2, 6), (3, 5, 4))):
            wait_bytes(ring_e.at[pl.ds(0, 4 * len(steps) - (1 - far))], table_sem.at[1 + far])
            for step in steps:
                rows = table.at[which, :, (z + step) % 8]
                remote(rows, rows, share_sem.at[0], share_sem.at[1], sibling).start()

    @pl.when(me < 31)
    def _():
        pl.semaphore_wait(plane_ready, 31 - me)

    @pl.when(core == 0)
    def _():
        h_pair.wait_recv()
        sum_h[...] = part_h[...] + in_h[...]
        scatter(sum_h, group_peers, ring_h, group_me)

    remote(kall.at[1 - x_lo], kall.at[1 - x_lo], k_sem.at[0], k_sem.at[1], partner).wait_recv()
    set_k(1 - x_lo)
    trig(1 - x_lo, 0, t_hi, t_lo, (1 - x_lo) * H, K + (1 - x_lo) * H, True)

    for name in ("wo", "width", "grad"):
        loads[name].wait()

    def add_pair(turn):
        pair = (y // 2 + turn) % 4
        cols = pl.ds(pl.multiple_of(pair * 256, 256), 256)
        for slot in (2 * pair, 2 * pair + 1):
            if turn:
                wait_bytes(cots.at[slot], cot_recv.at[slot])
            else:

                @pl.when(slot != y)
                def _(slot=slot):
                    wait_bytes(cots.at[slot], cot_recv.at[slot])

        block = jnp.concatenate([cots[2 * pair], cots[2 * pair + 1]], axis=1)
        both = jnp.concatenate(split(mask[0, :, cols] * dot(wo_ref[...], block, precision=exact)), axis=0)
        quants[1, :, cols] = both
        for sine in range(2):
            for i in range(4):
                rows = slice(sine * K + i * 128, sine * K + (i + 1) * 128)
                here = slice(i * 128, (i + 1) * 128)
                one = dot(t_hi[rows, cols], both, ((1,), (1,))) + dot(t_lo[rows, cols], both, ((1,), (1,)))
                sums_e[sine, here, :] = one + sums_e[sine, here, :] if turn else one

    for turn in (0, 1, 3, 2):
        add_pair(turn)

    def e_pair(q):
        rows = pl.ds(q * H, H)
        return remote(part_e.at[rows, :], in_e.at[rows, :], core_sem.at[0], core_sem.at[1], sibling)

    for q in range(2):
        rows = slice(q * H, (q + 1) * H)
        found = [sums_e[sine, rows, :] for sine in range(2)]
        found = [one + pltpu.roll(one, CH, 1) for one in found]
        part_e[rows, :] = jnp.where(low_lanes, found[0], found[1])

        @pl.when(core == 0)
        def _(q=q):
            e_pair(q).start()

    @pl.when(core == 1)
    def _():
        wait_bytes(in_e, core_sem.at[1])
        sum_e[...] = part_e[...] + in_e[...]
        scatter(sum_e, plane_peers, ring_e, place)

    @pl.when(core == 0)
    def _():
        gather(0, ring_h, 16)

    @pl.when(core == 1)
    def _():
        gather(1, ring_e, 32)

    def y_copy(which, other):
        return remote(
            out_y.at[which, other], in_y.at[which, y], y_sem.at[0, which], y_sem.at[1, which], on_y(other)
        )

    def fields(which):
        high, low = split(table[which].reshape(K, 128).T)
        left = jnp.concatenate(
            [
                jnp.concatenate([high[0:CH], high[CH:128]], axis=1),
                jnp.concatenate([low[0:CH], low[CH:128]], axis=1),
            ],
            axis=0,
        )
        for turn in (2, 1, 3, 0):
            at = (y // 2 + turn) % 4
            cols = pl.ds(pl.multiple_of(at * 256, 256), 256)
            both = dot(left, t_hi[:, cols]) + dot(left, t_lo[:, cols])
            field = both[0:CH] + both[CH:128]
            for n in range(2):
                other = 2 * at + n
                out_y[which, other] = field[:, n * S : (n + 1) * S]
                if turn:
                    y_copy(which, other).start()
                else:

                    @pl.when(other != y)
                    def _(other=other):
                        y_copy(which, other).start()

        in_y[which, y] = out_y[which, y]

    def forces(which, add):
        high, low = split(table[which].reshape(K, 128))
        high, low = high.astype(f32), low.astype(f32)
        sin_side = jnp.where(low_lanes, pltpu.roll(high, CH, 1), low).astype(bf16)
        cos_side = jnp.where(low_lanes, high, pltpu.roll(low, CH, 1)).astype(bf16)
        sin_side = jnp.concatenate([sin_side, sin_side], axis=1)
        cos_side = jnp.concatenate([cos_side, cos_side], axis=1)
        columns = [kcol[:, n : n + 1] for n in range(3)]
        for at in range(4):
            cols = slice(at * 256, (at + 1) * 256)
            high_q, low_q = quants[1 - which, 0:CH, cols], quants[1 - which, CH:128, cols]
            right = jnp.concatenate([high_q, high_q, low_q, low_q], axis=0)
            turn = cos_f[:, cols] * dot(sin_side, right) - sin_f[:, cols] * dot(cos_side, right)
            rows = [jnp.sum(column * turn, axis=0, keepdims=True) for column in columns]
            rows = jnp.concatenate(rows + [jnp.zeros((5, 256), f32)], axis=0)
            for half in range(2):
                slot = 2 * at + half
                here = rows[:, half * S : (half + 1) * S]
                out_f[slot] = out_f[slot] + here if add else here

    @pl.when(core == 0)
    def _():
        share(0)

    @pl.when(core == 1)
    def _():
        wait_bytes(table.at[0], share_sem.at[1])

    fields(0)
    forces(0, False)

    @pl.when(core == 1)
    def _():
        share(1)

    @pl.when(core == 0)
    def _():
        wait_bytes(table.at[1], share_sem.at[1])

    fields(1)
    forces(1, True)
    for other, device in y_peers:
        remote(out_f.at[other], in_f.at[y], f_sem.at[0], f_sem.at[1], device).start()
    in_f[y] = out_f[y]

    mine = mask[0, :, pl.ds(pl.multiple_of(y * S, S), S)]

    def collect(which):
        wait_bytes(in_y.at[which, pl.ds(0, 7)], y_sem.at[1, which])
        total = in_y[which, 0]
        for s in range(1, 8):
            total = total + in_y[which, s]
        return mine * total

    message_ref[...] = dot(wo_ref[...], collect(0), ((0,), (0,)), exact)
    wait_bytes(in_f.at[pl.ds(0, 7)], f_sem.at[1])
    total = in_f[0]
    for s in range(1, 8):
        total = total + in_f[s]
    force_ref[...] = (two_pi * total)[0:3, :]
    gfeat_ref[...] = dot(wq_ref[...], collect(1), precision=exact)

    k_copy.wait_send()
    wait_bytes(cots.at[pl.ds(0, 7)], cot_send)

    @pl.when(core == 0)
    def _():
        wait_bytes(in_e, core_sem.at[0])
        wait_bytes(ring_h.at[pl.ds(0, 15)], plane_sem.at[0])

    @pl.when(core == 1)
    def _():
        h_pair.wait_send()
        wait_bytes(ring_e.at[pl.ds(0, 31)], plane_sem.at[0])

    wait_bytes(ring_e.at[pl.ds(0, 31)], table_sem.at[0])
    wait_bytes(table.at[core], share_sem.at[0])
    for which in range(2):
        wait_bytes(in_y.at[which, pl.ds(0, 7)], y_sem.at[0, which])
    wait_bytes(in_f.at[pl.ds(0, 7)], f_sem.at[0])


def on_device(
    positions, feats, species, pad_count, k_lattice, filter_width, w_charge, species_embed, w_out, grad_out
):
    vmem = pl.BlockSpec(memory_space=pltpu.VMEM)
    dma = pltpu.SemaphoreType.DMA
    regular = pltpu.SemaphoreType.REGULAR
    operands = [
        pltpu.with_memory_space_constraint(array, pltpu.HBM)
        for array in (
            positions, feats, species.reshape(1, -1), pad_count, k_lattice, filter_width.reshape(1, -1),
            w_charge, species_embed.T, w_out, grad_out,
        )
    ]
    shapes = ((CH, S), (3, S), (CH, S))
    results = pl.pallas_call(
        kernel,
        out_shape=tuple(pltpu.VMEM(shape, f32) for shape in shapes),
        in_specs=[pl.BlockSpec(memory_space=pl.ANY)] * 10,
        out_specs=(vmem, vmem, vmem),
        scratch_shapes=[
            pltpu.VMEM((3, 2 * A), f32),
            pltpu.VMEM((CH, 2 * A), f32),
            pltpu.VMEM((1, 2 * A), jnp.int32),
            pltpu.SMEM((8,), jnp.int32),
            pltpu.VMEM((3, H), jnp.int32),
            pltpu.VMEM((1, CH), f32),
            pltpu.VMEM((CH, CH), f32),
            pltpu.VMEM((16, CH), f32),
            pltpu.VMEM((CH, CH), f32),
            pltpu.VMEM((2, 8, H), f32),
            pltpu.VMEM((K, 8), f32),
            pltpu.VMEM((K, 32), bf16),
            pltpu.VMEM((2, 32, A), bf16),
            pltpu.VMEM((2, 1, A), f32),
            pltpu.VMEM((2 * K, A), bf16),
            pltpu.VMEM((2 * K, A), bf16),
            pltpu.VMEM((2 * H, A), bf16),
            pltpu.VMEM((2 * H, A), bf16),
            pltpu.VMEM((K, A), f32),
            pltpu.VMEM((K, A), f32),
            pltpu.VMEM((2, 128, A), bf16),
            pltpu.VMEM((128, A), bf16),
            pltpu.VMEM((8, CH, S), f32),
            pltpu.VMEM((2, K, 128), f32),
            pltpu.VMEM((H, 128), f32),
            pltpu.VMEM((K, 128), f32),
            pltpu.VMEM((H, 128), f32),
            pltpu.VMEM((K, 128), f32),
            pltpu.VMEM((H, 128), f32),
            pltpu.VMEM((K, 128), f32),
            pltpu.VMEM((16, 16, 128), f32),
            pltpu.VMEM((32, 16, 128), f32),
            pltpu.VMEM((16, 128), f32),
            pltpu.VMEM((2, 4, 8, 16, 128), f32),
            pltpu.VMEM((2, 8, CH, S), f32),
            pltpu.VMEM((2, 8, CH, S), f32),
            pltpu.VMEM((8, 8, S), f32),
            pltpu.VMEM((8, 8, S), f32),
            dma((10,)), dma((2,)), dma, dma((8,)), dma((2,)),
            dma((2,)), dma((3,)), dma((2,)), dma((2, 2)), dma((2,)),
            regular((8,)), regular, regular, regular,
        ],
        name="ewald",
        compiler_params=pltpu.CompilerParams(
            collective_id=0, has_side_effects=True, vmem_limit_bytes=32 * 1024 * 1024
        ),
    )(*operands)
    return pl.pallas_call(
        put_away,
        out_shape=tuple(jax.ShapeDtypeStruct(shape, f32) for shape in shapes),
        in_specs=[vmem] * 3,
        out_specs=(pl.BlockSpec(memory_space=pl.ANY),) * 3,
        scratch_shapes=[dma((3,))],
        name="put_away",
        compiler_params=pltpu.CompilerParams(vmem_limit_bytes=1024 * 1024),
    )(*[pltpu.with_memory_space_constraint(array, pltpu.VMEM) for array in results])


def put_away(message, force, gfeat, message_out, force_out, gfeat_out, sem):
    copies = [
        pltpu.make_async_copy(src, dst, sem.at[n])
        for n, (src, dst) in enumerate(((message, message_out), (force, force_out), (gfeat, gfeat_out)))
    ]
    for copy in copies:
        copy.start()
    for copy in copies:
        copy.wait()


def solution(mesh):
    placed = (
        P(None, "atoms"),
        P(None, "atoms"),
        P("atoms"),
        P("atoms"),
        P(None, "kvec"),
        P(),
        P(),
        P(),
        P(),
        P(None, ("atoms", "kvec")),
    )
    return jax.shard_map(
        on_device,
        mesh=mesh,
        in_specs=placed,
        out_specs=(P(None, ("atoms", "kvec")),) * 3,
        check_vma=False,
    )
```

```python
import functools
import math

import jax
import jax.numpy as jnp
import numpy as np
from jax import lax
from jax.experimental import pallas as pl
from jax.experimental.pallas import tpu as pltpu
from jax.sharding import PartitionSpec as P

MESH = pl.DeviceIdType.MESH
exact = lax.Precision.HIGHEST
two_pi = 2.0 * math.pi
f32 = jnp.float32
bf16 = jnp.bfloat16

A = 1024
K = 512
H = 256
CH = 64
S = 128


def fit_poly(fn, count, points=2000):
    nodes = 0.25 * (np.cos(np.pi * (np.arange(points) + 0.5) / points) + 1.0) * 0.5
    table = np.vander(nodes / 0.25, count, increasing=True)
    coef = np.linalg.lstsq(table, fn(np.sqrt(nodes)), rcond=None)[0]
    return [float(c) / 0.25**n for n, c in enumerate(coef)]


sin_coef = fit_poly(lambda u: 2.0 * np.sin(np.pi * u) / u, 5)
cos_coef = fit_poly(lambda u: np.cos(np.pi * u), 5)


def horner(coef, sq):
    total = coef[-1]
    for c in coef[-2::-1]:
        total = total * sq + c
    return total


def sin_cos_turns(t):
    u = t - jnp.round(t)
    sq = u * u
    twice_sin = u * horner(sin_coef, sq)
    cos_half = horner(cos_coef, sq)
    return 1.0 - 0.5 * (twice_sin * twice_sin), twice_sin * cos_half


def split(value):
    high = value.astype(bf16)
    return high, (value - high.astype(f32)).astype(bf16)


def dot(a, b, dims=((1,), (0,)), precision=None):
    return lax.dot_general(a, b, (dims, ((), ())), precision=precision, preferred_element_type=f32)


def ring(d, n):
    return min(d, n - d)


y_steps = sorted(range(1, 8), key=lambda d: -ring(d, 8))
plane_steps = sorted(
    [(dx, dz) for dx in range(4) for dz in range(8) if dx or dz],
    key=lambda d: -(ring(d[0], 4) + ring(d[1], 8)),
)
plane_far = [int(ring(dz, 8) > 3) for _, dz in plane_steps]
y_order = (0, 1, 7, 2, 6, 3, 5, 4)


def kernel(
    pos_hbm, feats_hbm, species_hbm, pad_hbm, k_hbm, width_hbm, wq_hbm, embed_hbm, wo_hbm, grad_hbm,
    message_ref, force_ref, gfeat_ref,
    pos_ref, feats, species_ref, pad_ref, k_ref, width_ref, wq_ref, embed_ref, wo_ref,
    kall, kcol, kmat, xmat, mask, t_hi, t_lo, e_hi, e_lo, cos_f, sin_f, quants, far_charge, cots, sums_e,
    part_h, part_e, in_h, in_e, sum_h, sum_e, ring_h, ring_e, gain_ref, owned, table, out_y, in_y, out_f, in_f,
    load_sem, k_sem, cot_send, cot_recv, core_sem, plane_sem, table_sem, share_sem, y_sem, f_sem,
    y_ready, plane_ready, k_ready, core_ready,
):
    atoms_at = lax.axis_index("atoms")
    kvec_at = lax.axis_index("kvec")
    core, z, x_hi = atoms_at % 2, (atoms_at // 2) % 8, atoms_at // 16
    x_lo, y = kvec_at // 8, kvec_at % 8
    x = x_hi * 2 + x_lo
    me = z * 4 + x
    group_me = x_hi * 8 + z
    x_at = x_lo * 2 + x_hi
    place = x_at * 8 + z

    def on_y(other):
        return (atoms_at, x_lo * 8 + other)

    def on_plane(px, pz):
        return ((px // 2) * 16 + pz * 2 + core, (px % 2) * 8 + y)

    def on_start(p):
        return on_plane(p % 4, p // 4)

    y_peers = [((y + d) % 8, on_y((y + d) % 8)) for d in y_steps]
    plane_peers = []
    group_peers = []
    for dx, dz in plane_steps:
        px, pz = (x + dx) % 4, (z + dz) % 8
        plane_peers.append((((px % 2) * 2 + px // 2) * 8 + pz, on_plane(px, pz)))
        if dx % 2 == 0:
            group_peers.append(((px // 2) * 8 + pz, on_plane(px, pz)))
    sibling = (atoms_at + 1 - 2 * core, kvec_at)
    partner = (atoms_at, (1 - x_lo) * 8 + y)

    def remote(src, dst, send, recv, device):
        return pltpu.make_async_remote_copy(
            src_ref=src, dst_ref=dst, send_sem=send, recv_sem=recv, device_id=device, device_id_type=MESH
        )

    def signal(sem, device):
        pl.semaphore_signal(sem, inc=1, device_id=device, device_id_type=MESH)

    def wait_bytes(ref, sem):
        pltpu.make_async_copy(ref, ref, sem).wait()

    barrier = pltpu.get_barrier_semaphore()
    late = y // 5
    y_rank = (1 - late) * (2 * y - 1) + late * (16 - 2 * y)
    y_before = y_rank + (8 - y) // 8
    for i, other in enumerate(y_order):
        if i:

            @pl.when(i > y_rank)
            def _(other=other):
                signal(barrier, on_y(other))

    lax.fori_loop(me + 1, 32, lambda p, _: (signal(barrier, on_start(p)), 0)[1], 0)

    @pl.when(core == 1)
    def _():
        signal(barrier, sibling)

    loads = {}
    for n, (name, src, dst) in enumerate([
        ("k", k_hbm, k_ref),
        ("pos", pos_hbm, pos_ref),
        ("pad", pad_hbm, pad_ref),
        ("feats", feats_hbm, feats),
        ("species", species_hbm, species_ref),
        ("wq", wq_hbm, wq_ref),
        ("embed", embed_hbm, embed_ref),
        ("wo", wo_hbm, wo_ref),
        ("width", width_hbm, width_ref),
        ("grad", grad_hbm, cots.at[y]),
    ]):
        loads[name] = pltpu.make_async_copy(src, dst, load_sem.at[n])
        loads[name].start()

    before = y_before + me + 1 - core

    @pl.when(before > 0)
    def _():
        pl.semaphore_wait(barrier, before)

    for i, other in enumerate(y_order[:-1]):

        @pl.when(i < y_rank)
        def _(other=other):
            signal(y_ready.at[y], on_y(other))

    @pl.when(x_lo == 1)
    def _():
        signal(k_ready, partner)

    def cot_copy(device):
        return remote(grad_hbm, cots.at[y], cot_send, cot_recv.at[y], device)

    for i, other in enumerate(y_order[:-1]):

        @pl.when(i < y_rank)
        def _(other=other):
            cot_copy(on_y(other)).start()

    @pl.when(core == 0)
    def _():
        signal(core_ready, sibling)

    loads["k"].wait()
    kall[x_lo] = jnp.concatenate([k_ref[...].astype(f32), jnp.zeros((5, H), f32)], axis=0)
    k_copy = remote(kall.at[x_lo], kall.at[x_lo], k_sem.at[0], k_sem.at[1], partner)

    @pl.when(x_lo == 1)
    def _():
        k_copy.start()

    lax.fori_loop(0, me, lambda p, _: (signal(plane_ready, on_start(p)), 0)[1], 0)

    halves = [pl.ds(pl.multiple_of(h * A, A), A) for h in (x_lo, 1 - x_lo)]
    loads["pos"].wait()
    loads["pad"].wait()
    lanes = lax.broadcasted_iota(jnp.int32, (1, 256), 1)
    for n, h in enumerate((x_lo, 1 - x_lo)):
        pos = jnp.concatenate([pos_ref[:, halves[n]], jnp.zeros((5, A), f32)], axis=0)
        pos_hi = pos.astype(bf16).astype(f32)
        pos_mid = (pos - pos_hi).astype(bf16).astype(f32)
        pos_low = (pos - pos_hi) - pos_mid
        xmat[n] = jnp.concatenate([pos_hi, pos_mid, pos_low, jnp.zeros((8, A), f32)], axis=0).astype(bf16)
        for block in range(4):
            mask[n, :, block * 256 : (block + 1) * 256] = (lanes < pad_ref[h * 4 + block]).astype(f32)

    def set_k(q):
        kt = kall[q].T
        kcol[pl.ds(pl.multiple_of(q * H, H), H), :] = kt
        kmat[pl.ds(pl.multiple_of(q * H, H), H), :] = jnp.concatenate([kt] * 4, axis=1).astype(bf16)

    def trig(q, n, high_ref, low_ref, cos_base, sin_base, keep):
        def step(i, _):
            rows = pl.ds(pl.multiple_of(q * H + i * 128, 128), 128)
            cos_rows = pl.ds(pl.multiple_of(cos_base + i * 128, 128), 128)
            sin_rows = pl.ds(pl.multiple_of(sin_base + i * 128, 128), 128)
            left = kmat[rows, :]
            for at in range(4):
                cols = slice(at * 256, (at + 1) * 256)
                cos, sin = sin_cos_turns(dot(left, xmat[n, :, cols]))
                if keep:
                    cos_f[rows, cols] = cos
                    sin_f[rows, cols] = sin
                high_ref[cos_rows, cols], low_ref[cos_rows, cols] = split(cos)
                high_ref[sin_rows, cols], low_ref[sin_rows, cols] = split(sin)
            return 0

        lax.fori_loop(0, H // 128, step, 0)

    low_lanes = lax.broadcasted_iota(jnp.int32, (1, 128), 1) < CH

    def factors(out_ref, base, terms):
        for i in range(2):
            found = []
            for sine in (0, 1):
                one = jnp.zeros((128, 128), f32)
                for high_ref, low_ref, cos_base, sin_base, quant in terms:
                    rows = pl.ds(pl.multiple_of((sin_base if sine else cos_base) + i * 128, 128), 128)
                    one = one + dot(high_ref[rows, :], quant[...], ((1,), (1,)))
                    one = one + dot(low_ref[rows, :], quant[...], ((1,), (1,)))
                found.append(one + pltpu.roll(one, CH, 1))
            out_ref[pl.ds(pl.multiple_of(base + i * 128, 128), 128), :] = jnp.where(low_lanes, found[0], found[1])

    set_k(x_lo)
    trig(x_lo, 0, t_hi, t_lo, x_lo * H, K + x_lo * H, True)

    @pl.when(x_lo == 0)
    def _():
        pl.semaphore_wait(k_ready, 1)
        k_copy.start()

    for i, other in enumerate(y_order):
        if i:

            @pl.when(i > y_rank)
            def _(other=other):
                pl.semaphore_wait(y_ready.at[other], 1)
                cot_copy(on_y(other)).start()

    for name in ("feats", "species", "wq", "embed"):
        loads[name].wait()
    for n, quant in enumerate((quants.at[0], far_charge)):
        one_hot = (lax.broadcasted_iota(jnp.int32, (16, A), 0) == species_ref[:, halves[n]]).astype(f32)
        quant[0:CH, :], quant[CH:128, :] = split(
            mask[n]
            * (
                dot(wq_ref[...], feats[:, halves[n]], ((0,), (0,)), exact)
                + dot(embed_ref[...], one_hot, ((0,), (0,)), exact)
            )
        )

    trig(x_lo, 1, e_hi, e_lo, 0, H, False)
    factors(
        part_h, 0, [(t_hi, t_lo, x_lo * H, K + x_lo * H, quants.at[0]), (e_hi, e_lo, 0, H, far_charge)]
    )

    h_pair = remote(part_h, in_h, core_sem.at[0], core_sem.at[1], sibling)

    @pl.when(core == 1)
    def _():
        pl.semaphore_wait(core_ready, 1)
        h_pair.start()

    def gain_of(first):
        wave = two_pi * kcol[pl.ds(pl.multiple_of(first, 16), 16), :]
        square = jnp.sum(wave * wave, axis=1, keepdims=True)
        width = width_ref[...]
        width = jnp.concatenate([width, width], axis=1)
        return jnp.exp(-square * width) * 40.0 / (square + 40.0) / 256.0

    def scatter(total, peers, ring_ref, mine):
        for p, device in peers:
            remote(
                total.at[pl.ds(pl.multiple_of(p * 16, 16), 16), :], ring_ref.at[mine],
                plane_sem.at[0], plane_sem.at[1], device,
            ).start()
        ring_ref[mine] = total[pl.ds(pl.multiple_of(mine * 16, 16), 16), :]

    def gather(which, ring_ref, count):
        gain_ref[...] = gain_of(place * 16)
        wait_bytes(ring_ref.at[pl.ds(0, count - 1)], plane_sem.at[1])
        total = ring_ref[0]
        for p in range(1, count):
            total = total + ring_ref[p]
        owned[...] = gain_ref[...] * total
        for (_, device), far in zip(plane_peers, plane_far):
            remote(owned, table.at[which, x_at, z], table_sem.at[0], table_sem.at[1 + far], device).start()
        table[which, x_at, z] = owned[...]

    def share(which):
        for far, steps in enumerate(((0, 1, 7, 2, 6, 3, 5), (4,))):
            wait_bytes(ring_e.at[pl.ds(0, 4 * len(steps) - (1 - far))], table_sem.at[1 + far])
            for step in steps:
                rows = table.at[which, :, (z + step) % 8]
                remote(rows, rows, share_sem.at[0], share_sem.at[1], sibling).start()

    @pl.when(me < 31)
    def _():
        pl.semaphore_wait(plane_ready, 31 - me)

    @pl.when(core == 0)
    def _():
        h_pair.wait_recv()
        sum_h[...] = part_h[...] + in_h[...]
        scatter(sum_h, group_peers, ring_h, group_me)

    remote(kall.at[1 - x_lo], kall.at[1 - x_lo], k_sem.at[0], k_sem.at[1], partner).wait_recv()
    set_k(1 - x_lo)
    trig(1 - x_lo, 0, t_hi, t_lo, (1 - x_lo) * H, K + (1 - x_lo) * H, True)

    for name in ("wo", "width", "grad"):
        loads[name].wait()

    def add_pair(turn):
        pair = (y // 2 + turn) % 4
        cols = pl.ds(pl.multiple_of(pair * 256, 256), 256)
        for slot in (2 * pair, 2 * pair + 1):
            if turn:
                wait_bytes(cots.at[slot], cot_recv.at[slot])
            else:

                @pl.when(slot != y)
                def _(slot=slot):
                    wait_bytes(cots.at[slot], cot_recv.at[slot])

        block = jnp.concatenate([cots[2 * pair], cots[2 * pair + 1]], axis=1)
        both = jnp.concatenate(split(mask[0, :, cols] * dot(wo_ref[...], block, precision=exact)), axis=0)
        quants[1, :, cols] = both
        for sine in range(2):
            for i in range(4):
                rows = slice(sine * K + i * 128, sine * K + (i + 1) * 128)
                here = slice(i * 128, (i + 1) * 128)
                one = dot(t_hi[rows, cols], both, ((1,), (1,))) + dot(t_lo[rows, cols], both, ((1,), (1,)))
                sums_e[sine, here, :] = one + sums_e[sine, here, :] if turn else one

    for turn in (0, 1, 3, 2):
        add_pair(turn)

    def e_pair(q):
        rows = pl.ds(q * H, H)
        return remote(part_e.at[rows, :], in_e.at[rows, :], core_sem.at[0], core_sem.at[1], sibling)

    for q in range(2):
        rows = slice(q * H, (q + 1) * H)
        found = [sums_e[sine, rows, :] for sine in range(2)]
        found = [one + pltpu.roll(one, CH, 1) for one in found]
        part_e[rows, :] = jnp.where(low_lanes, found[0], found[1])

        @pl.when(core == 0)
        def _(q=q):
            e_pair(q).start()

    @pl.when(core == 1)
    def _():
        wait_bytes(in_e, core_sem.at[1])
        sum_e[...] = part_e[...] + in_e[...]
        scatter(sum_e, plane_peers, ring_e, place)

    @pl.when(core == 0)
    def _():
        gather(0, ring_h, 16)

    @pl.when(core == 1)
    def _():
        gather(1, ring_e, 32)

    def y_copy(which, other):
        return remote(
            out_y.at[which, other], in_y.at[which, y], y_sem.at[0, which], y_sem.at[1, which], on_y(other)
        )

    def fields(which):
        high, low = split(table[which].reshape(K, 128).T)
        left = jnp.concatenate(
            [
                jnp.concatenate([high[0:CH], high[CH:128]], axis=1),
                jnp.concatenate([low[0:CH], low[CH:128]], axis=1),
            ],
            axis=0,
        )
        for turn in (2, 1, 3, 0):
            at = (y // 2 + turn) % 4
            cols = pl.ds(pl.multiple_of(at * 256, 256), 256)
            both = dot(left, t_hi[:, cols]) + dot(left, t_lo[:, cols])
            field = both[0:CH] + both[CH:128]
            for n in range(2):
                other = 2 * at + n
                out_y[which, other] = field[:, n * S : (n + 1) * S]
                if turn:
                    y_copy(which, other).start()
                else:

                    @pl.when(other != y)
                    def _(other=other):
                        y_copy(which, other).start()

        in_y[which, y] = out_y[which, y]

    def forces(which, add):
        high, low = split(table[which].reshape(K, 128))
        high, low = high.astype(f32), low.astype(f32)
        sin_side = jnp.where(low_lanes, pltpu.roll(high, CH, 1), low).astype(bf16)
        cos_side = jnp.where(low_lanes, high, pltpu.roll(low, CH, 1)).astype(bf16)
        sin_side = jnp.concatenate([sin_side, sin_side], axis=1)
        cos_side = jnp.concatenate([cos_side, cos_side], axis=1)
        columns = [kcol[:, n : n + 1] for n in range(3)]
        for at in range(4):
            cols = slice(at * 256, (at + 1) * 256)
            high_q, low_q = quants[1 - which, 0:CH, cols], quants[1 - which, CH:128, cols]
            right = jnp.concatenate([high_q, high_q, low_q, low_q], axis=0)
            turn = cos_f[:, cols] * dot(sin_side, right) - sin_f[:, cols] * dot(cos_side, right)
            rows = [jnp.sum(column * turn, axis=0, keepdims=True) for column in columns]
            rows = jnp.concatenate(rows + [jnp.zeros((5, 256), f32)], axis=0)
            for half in range(2):
                slot = 2 * at + half
                here = rows[:, half * S : (half + 1) * S]
                out_f[slot] = out_f[slot] + here if add else here

    @pl.when(core == 0)
    def _():
        share(0)

    @pl.when(core == 1)
    def _():
        wait_bytes(table.at[0], share_sem.at[1])

    fields(0)
    forces(0, False)

    @pl.when(core == 1)
    def _():
        share(1)

    @pl.when(core == 0)
    def _():
        wait_bytes(table.at[1], share_sem.at[1])

    fields(1)
    forces(1, True)
    for other, device in y_peers:
        remote(out_f.at[other], in_f.at[y], f_sem.at[0], f_sem.at[1], device).start()
    in_f[y] = out_f[y]

    mine = mask[0, :, pl.ds(pl.multiple_of(y * S, S), S)]

    def collect(which):
        wait_bytes(in_y.at[which, pl.ds(0, 7)], y_sem.at[1, which])
        total = in_y[which, 0]
        for s in range(1, 8):
            total = total + in_y[which, s]
        return mine * total

    message_ref[...] = dot(wo_ref[...], collect(0), ((0,), (0,)), exact)
    wait_bytes(in_f.at[pl.ds(0, 7)], f_sem.at[1])
    total = in_f[0]
    for s in range(1, 8):
        total = total + in_f[s]
    force_ref[...] = (two_pi * total)[0:3, :]
    gfeat_ref[...] = dot(wq_ref[...], collect(1), precision=exact)

    k_copy.wait_send()
    wait_bytes(cots.at[pl.ds(0, 7)], cot_send)

    @pl.when(core == 0)
    def _():
        wait_bytes(in_e, core_sem.at[0])
        wait_bytes(ring_h.at[pl.ds(0, 15)], plane_sem.at[0])

    @pl.when(core == 1)
    def _():
        h_pair.wait_send()
        wait_bytes(ring_e.at[pl.ds(0, 31)], plane_sem.at[0])

    wait_bytes(ring_e.at[pl.ds(0, 31)], table_sem.at[0])
    wait_bytes(table.at[core], share_sem.at[0])
    for which in range(2):
        wait_bytes(in_y.at[which, pl.ds(0, 7)], y_sem.at[0, which])
    wait_bytes(in_f.at[pl.ds(0, 7)], f_sem.at[0])


def on_device(
    positions, feats, species, pad_count, k_lattice, filter_width, w_charge, species_embed, w_out, grad_out
):
    vmem = pl.BlockSpec(memory_space=pltpu.VMEM)
    dma = pltpu.SemaphoreType.DMA
    regular = pltpu.SemaphoreType.REGULAR
    operands = [
        pltpu.with_memory_space_constraint(array, pltpu.HBM)
        for array in (
            positions, feats, species.reshape(1, -1), pad_count, k_lattice, filter_width.reshape(1, -1),
            w_charge, species_embed.T, w_out, grad_out,
        )
    ]
    shapes = ((CH, S), (3, S), (CH, S))
    results = pl.pallas_call(
        kernel,
        out_shape=tuple(pltpu.VMEM(shape, f32) for shape in shapes),
        in_specs=[pl.BlockSpec(memory_space=pl.ANY)] * 10,
        out_specs=(vmem, vmem, vmem),
        scratch_shapes=[
            pltpu.VMEM((3, 2 * A), f32),
            pltpu.VMEM((CH, 2 * A), f32),
            pltpu.VMEM((1, 2 * A), jnp.int32),
            pltpu.SMEM((8,), jnp.int32),
            pltpu.VMEM((3, H), jnp.int32),
            pltpu.VMEM((1, CH), f32),
            pltpu.VMEM((CH, CH), f32),
            pltpu.VMEM((16, CH), f32),
            pltpu.VMEM((CH, CH), f32),
            pltpu.VMEM((2, 8, H), f32),
            pltpu.VMEM((K, 8), f32),
            pltpu.VMEM((K, 32), bf16),
            pltpu.VMEM((2, 32, A), bf16),
            pltpu.VMEM((2, 1, A), f32),
            pltpu.VMEM((2 * K, A), bf16),
            pltpu.VMEM((2 * K, A), bf16),
            pltpu.VMEM((2 * H, A), bf16),
            pltpu.VMEM((2 * H, A), bf16),
            pltpu.VMEM((K, A), f32),
            pltpu.VMEM((K, A), f32),
            pltpu.VMEM((2, 128, A), bf16),
            pltpu.VMEM((128, A), bf16),
            pltpu.VMEM((8, CH, S), f32),
            pltpu.VMEM((2, K, 128), f32),
            pltpu.VMEM((H, 128), f32),
            pltpu.VMEM((K, 128), f32),
            pltpu.VMEM((H, 128), f32),
            pltpu.VMEM((K, 128), f32),
            pltpu.VMEM((H, 128), f32),
            pltpu.VMEM((K, 128), f32),
            pltpu.VMEM((16, 16, 128), f32),
            pltpu.VMEM((32, 16, 128), f32),
            pltpu.VMEM((16, 128), f32),
            pltpu.VMEM((16, 128), f32),
            pltpu.VMEM((2, 4, 8, 16, 128), f32),
            pltpu.VMEM((2, 8, CH, S), f32),
            pltpu.VMEM((2, 8, CH, S), f32),
            pltpu.VMEM((8, 8, S), f32),
            pltpu.VMEM((8, 8, S), f32),
            dma((10,)), dma((2,)), dma, dma((8,)), dma((2,)),
            dma((2,)), dma((3,)), dma((2,)), dma((2, 2)), dma((2,)),
            regular((8,)), regular, regular, regular,
        ],
        name="ewald",
        compiler_params=pltpu.CompilerParams(
            collective_id=0, has_side_effects=True, vmem_limit_bytes=32 * 1024 * 1024
        ),
    )(*operands)
    return pl.pallas_call(
        put_away,
        out_shape=tuple(jax.ShapeDtypeStruct(shape, f32) for shape in shapes),
        in_specs=[vmem] * 3,
        out_specs=(pl.BlockSpec(memory_space=pl.ANY),) * 3,
        scratch_shapes=[dma((3,))],
        name="put_away",
        compiler_params=pltpu.CompilerParams(vmem_limit_bytes=1024 * 1024),
    )(*[pltpu.with_memory_space_constraint(array, pltpu.VMEM) for array in results])


def put_away(message, force, gfeat, message_out, force_out, gfeat_out, sem):
    copies = [
        pltpu.make_async_copy(src, dst, sem.at[n])
        for n, (src, dst) in enumerate(((message, message_out), (force, force_out), (gfeat, gfeat_out)))
    ]
    for copy in copies:
        copy.start()
    for copy in copies:
        copy.wait()


def solution(mesh):
    placed = (
        P(None, "atoms"),
        P(None, "atoms"),
        P("atoms"),
        P("atoms"),
        P(None, "kvec"),
        P(),
        P(),
        P(),
        P(),
        P(None, ("atoms", "kvec")),
    )
    return jax.shard_map(
        on_device,
        mesh=mesh,
        in_specs=placed,
        out_specs=(P(None, ("atoms", "kvec")),) * 3,
        check_vma=False,
    )
```
